32 devices in a mesh: grp: 2 (over x), tm: 16 (over z, y, core).
Axes of the slice: x: 2, y: 2, z: 4, core: 2. Of those that a mesh axis runs over, the one named last changes fastest.
Arguments:
- upsampled: bfloat16 [2, 12288, 512], P(None, ('grp', 'tm')), parts along dimension 1, may hold values from -6 to 6
- taps: bfloat16 [3, 7, 512, 512], replicated, may hold values from -0.09375 to 0.09375
- bias_wide: float32 [3, 512], replicated, may hold values from -1.8 to 1.8
- pointwise: bfloat16 [3, 512, 512], replicated, may hold values from -0.25 to 0.25
- bias_point: float32 [3, 512], replicated, may hold values from -1.8 to 1.8
- alpha_in: float32 [3, 512], replicated, may hold values from 0.5 to 4
- beta_in: float32 [3, 512], replicated, may hold values from 0.5 to 4
- alpha_mid: float32 [3, 512], replicated, may hold values from 0.5 to 4
- beta_mid: float32 [3, 512], replicated, may hold values from 0.5 to 4
Outputs:
- decoded: bfloat16 [12288, 512], P(('grp', 'tm')), parts along dimension 0
The draws below stay inside these ranges and needn't reach their ends.
There are 2 independent parts, one for each index of `grp`. The reference program is written for one: setup_inputs(seed, part) draws one part's arguments, and reference() takes and returns one part's arrays. A program takes and returns all parts, laid end to end along the dimension named above; an argument that names none is the same for every part. Nothing has to cross between parts.
All inputs are finite; a program needn't handle non-finite values.
Results may differ from the reference program's by a relative error of at most 0.027.
The reference program's roundings to bfloat16 on the way count: a program that leaves them out, or rounds other values in their place, can miss the bound.
Values may be sent and summed in bfloat16 or wider, within the bound.
No kernel may reach another device: no remote copies, remote signals or barrier semaphores. Data moves between devices by JAX's collectives and lax.ppermute only.
A program may use at most 128 MiB of HBM per device.

```python
import math
import jax
import jax.numpy as jnp

C = 512
KERNEL = 7
STRIDE = 8
UNITS = 3
FRAMES = 6144


def block_levels(stream_key, dims, shards, smallest, high):
    def one(position, parts):
        draws = jax.random.uniform(jax.random.fold_in(jax.random.fold_in(stream_key, 6), position), (parts,), jnp.float32, smallest / len(shards), high / len(shards))
        return jnp.repeat(jnp.exp(draws), dims[position] // parts).reshape((-1,) + (1,) * (len(dims) - position - 1))

    gain = one(*shards[0])
    for cut in shards[1:]:
        gain = gain * one(*cut)
    return gain


def noise(own_key, extent, deviation, most, shards=(), kind=jnp.bfloat16):
    loudness = block_levels(own_key, extent, shards, -0.22, 0.18) if shards else 1.0
    array = jax.random.normal(own_key, extent, jnp.float32) * deviation * loudness
    return jnp.minimum(jnp.maximum(array, -most), most).astype(kind)


def setup_inputs(seed: int = 0, part: int = 0) -> dict:
    key_list = jax.random.split(jax.random.key(seed), 10)
    part_keys = jax.random.split(jax.random.fold_in(key_list[9], part), 10)
    return {
        "upsampled": noise(part_keys[0], (2, FRAMES, C), 1.0, 6.0, ((1, 16),)),
        "taps": noise(key_list[1], (UNITS, KERNEL, C, C), (KERNEL * C) ** -0.5, 0.09375),
        "bias_wide": noise(key_list[2], (UNITS, C), 0.3, 1.8, (), jnp.float32),
        "pointwise": noise(key_list[3], (UNITS, C, C), C ** -0.5, 0.25),
        "bias_point": noise(key_list[4], (UNITS, C), 0.3, 1.8, (), jnp.float32),
        "alpha_in": jnp.clip(jnp.exp(jax.random.uniform(key_list[5], (UNITS, C), jnp.float32, math.log(0.5), math.log(4.0))), 0.5, 4.0),
        "beta_in": jnp.clip(jnp.exp(jax.random.uniform(key_list[6], (UNITS, C), jnp.float32, math.log(0.5), math.log(4.0))), 0.5, 4.0),
        "alpha_mid": jnp.clip(jnp.exp(jax.random.uniform(key_list[7], (UNITS, C), jnp.float32, math.log(0.5), math.log(4.0))), 0.5, 4.0),
        "beta_mid": jnp.clip(jnp.exp(jax.random.uniform(key_list[8], (UNITS, C), jnp.float32, math.log(0.5), math.log(4.0))), 0.5, 4.0),
    }


def snake(values, alpha, beta):
    return values + jnp.square(jnp.sin(alpha * values)) / beta


def residual_unit(inputs, dilation, taps, bias_wide, pointwise, bias_point, alpha_in, beta_in, alpha_mid, beta_mid):
    length = inputs.shape[0] - 6 * dilation
    widened = snake(inputs.astype(jnp.float32), alpha_in, beta_in).astype(jnp.bfloat16)
    middle = jnp.zeros((length, taps.shape[2]), jnp.float32) + bias_wide
    for k in range(KERNEL):
        middle = middle + jnp.dot(widened[k * dilation:k * dilation + length], taps[k], preferred_element_type=jnp.float32)
    gated = snake(middle, alpha_mid, beta_mid).astype(jnp.bfloat16)
    update = jnp.dot(gated, pointwise, preferred_element_type=jnp.float32) + bias_point
    kept = inputs[3 * dilation:3 * dilation + length].astype(jnp.float32)
    return (kept + update).astype(jnp.bfloat16)


def reference(upsampled, taps, bias_wide, pointwise, bias_point, alpha_in, beta_in, alpha_mid, beta_mid):
    frames = upsampled.shape[1]
    shifted = jnp.concatenate([jnp.zeros((STRIDE, upsampled.shape[2]), upsampled.dtype), upsampled[1, :frames - STRIDE]], axis=0)
    current = (upsampled[0].astype(jnp.float32) + shifted.astype(jnp.float32)).astype(jnp.bfloat16)
    dilations = (1, 3, 9)
    for index in range(UNITS):
        spread = 3 * dilations[index]
        padded = jnp.pad(current, ((spread, spread), (0, 0)))
        current = residual_unit(padded, dilations[index], taps[index], bias_wide[index], pointwise[index], bias_point[index], alpha_in[index], beta_in[index], alpha_mid[index], beta_mid[index])
    return current
```

```python
import functools
import math

import jax
import jax.numpy as jnp
import numpy as np
from jax import lax
from jax.experimental import pallas as pl
from jax.experimental.pallas import tpu as pltpu
from jax.sharding import PartitionSpec as P

KERNEL = 7
STRIDE = 8
UNITS = 3
DILATIONS = (1, 3, 9)
LANES = 128
LEFT = 48
SENT = 48
HALO = 40
SEGMENTS = 16

SINE = (9.86952481, -32.46513948, 42.64342537, -29.42627071, 10.5812946)


def snake(values, frequency, inverse):
    turns = values * frequency
    rest = turns - jnp.round(turns)
    square = rest * rest
    sine = jnp.float32(SINE[4])
    for coefficient in SINE[3::-1]:
        sine = sine * square + jnp.float32(coefficient)
    return values + (sine * square) * inverse


def rounded(values):
    return values.astype(jnp.bfloat16).astype(jnp.float32)


def segment_plan(frames):
    plan = []
    for unit in range(UNITS):
        reach = 3 * sum(DILATIONS[unit + 1 :])
        first = -(-reach // 8) * 8
        length = -(-(frames + 2 * first) // SEGMENTS)
        if length % 8 == 0 and unit == UNITS - 1:
            length += 1
        plan.append((-first, length))
    return plan


def kernel(
    frames, tracks,
    up, from_chip, from_next, bias_wide, bias_point, alpha_in, beta_in, alpha_mid, beta_mid,
    point_hbm, taps_hbm,
    out,
    x_rows, s_rows, tiles, taps, point, sems,
):
    channels = out.shape[1]
    groups = channels // LANES
    copies = []
    for unit in range(UNITS):
        row = []
        for k in range(KERNEL):
            row.append(
                pltpu.make_async_copy(taps_hbm.at[unit, k], taps.at[unit, k], sems.at[unit, k])
            )
        row.append(pltpu.make_async_copy(point_hbm.at[unit], point.at[unit], sems.at[unit, KERNEL]))
        for copy in row:
            copy.start()
        copies.append(row)

    place = lax.axis_index("tm")
    odd = place % 2 == 1
    is_first = place == 0
    is_last = place == tracks - 1
    rows = frames + 2 * LEFT

    def lane(c):
        return slice(c * LANES, (c + 1) * LANES)

    def snake_in(unit, c):
        frequency = alpha_in[unit : unit + 1, lane(c)] * (1.0 / math.pi)
        inverse = 1.0 / beta_in[unit : unit + 1, lane(c)]
        return lambda v: snake(v, frequency, inverse)

    def clear_outside(c):
        low = s_rows[c, 0:LEFT, :]
        s_rows[c, 0:LEFT, :] = jnp.where(is_first, 0.0, low)
        high = s_rows[c, LEFT + frames :, :]
        s_rows[c, LEFT + frames :, :] = jnp.where(is_last, 0.0, high)

    for c in range(groups):
        chip = from_chip[:, lane(c)].astype(jnp.float32)
        other = from_next[:, lane(c)].astype(jnp.float32)
        low = jnp.where(odd, chip, other)
        high = jnp.where(odd, other, chip)
        carried = jnp.where(is_first, 0.0, low[HALO:SENT])
        own = up[0, :, lane(c)].astype(jnp.float32)
        later = up[1, :, lane(c)].astype(jnp.float32)
        middle = rounded(own + jnp.concatenate([carried, later[: frames - STRIDE]], axis=0))
        joint = rounded(high[:STRIDE] + later[frames - STRIDE :])
        current = jnp.concatenate([low[:HALO], middle, joint, high[STRIDE:HALO]], axis=0)
        edge = LEFT - HALO
        x_rows[c, edge : rows - edge, :] = current
        s_rows[c, edge : rows - edge, :] = snake_in(0, c)(current)
        clear_outside(c)

    for unit in range(UNITS):
        dilation = DILATIONS[unit]
        first, length = segment_plan(frames)[unit]
        base = LEFT + first
        for j in range(length + 6 * dilation):
            start = base - 3 * dilation + j
            for c in range(groups):
                low = s_rows[c, pl.ds(start, 8, stride=length), :]
                high = s_rows[c, pl.ds(start + 8 * length, 8, stride=length), :]
                tiles[j * SEGMENTS : (j + 1) * SEGMENTS, lane(c)] = jnp.concatenate(
                    [low, high], axis=0
                ).astype(jnp.bfloat16)
        cut = -(-length // 2)
        for begin, end in ((0, cut), (cut, length)):
            middle = None
            for k in range(KERNEL):
                if begin == 0:
                    copies[unit][k].wait()
                window = tiles[
                    (begin + k * dilation) * SEGMENTS : (end + k * dilation) * SEGMENTS, :
                ]
                product = jnp.dot(window, taps[unit, k], preferred_element_type=jnp.float32)
                middle = product if middle is None else middle + product
            frequency = alpha_mid[unit : unit + 1, :] * (1.0 / math.pi)
            inverse = 1.0 / beta_mid[unit : unit + 1, :]
            gated = snake(middle + bias_wide[unit : unit + 1, :], frequency, inverse)
            if begin == 0:
                copies[unit][KERNEL].wait()
            update = jnp.dot(
                gated.astype(jnp.bfloat16), point[unit], preferred_element_type=jnp.float32
            ) + bias_point[unit : unit + 1, :]
            for c in range(groups):
                for j in range(begin, end):
                    row = (j - begin) * SEGMENTS
                    for half in range(2):
                        where = pl.ds(base + j + half * 8 * length, 8, stride=length)
                        change = update[row + half * 8 : row + half * 8 + 8, lane(c)]
                        current = rounded(x_rows[c, where, :] + change)
                        x_rows[c, where, :] = current
                        if unit + 1 < UNITS:
                            s_rows[c, where, :] = snake_in(unit + 1, c)(current)
        if unit + 1 < UNITS:
            for c in range(groups):
                clear_outside(c)

    for c in range(groups):
        out[:, lane(c)] = x_rows[c, LEFT : LEFT + frames, :].astype(jnp.bfloat16)


def swaps(groups, count):
    near, far = [], []
    for group in range(groups):
        for place in range(count):
            me = group * count + place
            near.append((me, group * count + (place ^ 1)))
            if place == 0 or place == count - 1:
                partner = group ^ 1
                far.append((me, partner * count + place))
            else:
                far.append((me, me + 1 if place % 2 else me - 1))
    return near, far


def per_device(
    upsampled, taps, bias_wide, pointwise, bias_point, alpha_in, beta_in, alpha_mid, beta_mid
):
    frames, channels = upsampled.shape[1:]
    count = lax.axis_size("tm")
    near, far = swaps(lax.axis_size("grp"), count)

    def summed(own, later):
        return (own.astype(jnp.float32) + later.astype(jnp.float32)).astype(jnp.bfloat16)

    none = jnp.zeros((STRIDE, channels), upsampled.dtype)
    to_next = summed(
        jnp.concatenate([upsampled[0, frames - HALO :], none], axis=0),
        upsampled[1, frames - SENT :],
    )
    to_last = summed(
        upsampled[0, :SENT], jnp.concatenate([none, upsampled[1, : SENT - STRIDE]], axis=0)
    )
    even = lax.axis_index("tm") % 2 == 0
    from_next = lax.ppermute(jnp.where(even, to_last, to_next), ("grp", "tm"), far)
    from_chip = lax.ppermute(jnp.where(even, to_next, to_last), ("grp", "tm"), near)

    rows = frames + 2 * LEFT
    reach = max(
        length + 6 * dilation
        for (_, length), dilation in zip(segment_plan(frames), DILATIONS)
    )
    vmem = pl.BlockSpec(memory_space=pltpu.VMEM)
    hbm = pl.BlockSpec(memory_space=pl.ANY)
    return pl.pallas_call(
        functools.partial(kernel, frames, count),
        out_shape=jax.ShapeDtypeStruct((frames, channels), jnp.bfloat16),
        in_specs=[vmem] * 9 + [hbm] * 2,
        out_specs=vmem,
        scratch_shapes=[
            pltpu.VMEM((channels // LANES, rows, LANES), jnp.float32),
            pltpu.VMEM((channels // LANES, rows, LANES), jnp.float32),
            pltpu.VMEM((reach * SEGMENTS, channels), jnp.bfloat16),
            pltpu.VMEM(taps.shape, jnp.bfloat16),
            pltpu.VMEM(pointwise.shape, jnp.bfloat16),
            pltpu.SemaphoreType.DMA((UNITS, KERNEL + 1)),
        ],
        compiler_params=pltpu.CompilerParams(vmem_limit_bytes=40 * 2**20),
        name="units",
    )(
        upsampled, from_chip, from_next, bias_wide, bias_point,
        alpha_in, beta_in, alpha_mid, beta_mid, pointwise, taps,
    )


def solution(mesh):
    placed = (P(None, ("grp", "tm"), None), P(), P(), P(), P(), P(), P(), P(), P())
    return jax.shard_map(
        per_device, mesh=mesh, in_specs=placed, out_specs=P(("grp", "tm"), None), check_vma=False
    )
```

```python
import functools
import math

import jax
import jax.numpy as jnp
from jax import lax
from jax.experimental import pallas as pl
from jax.experimental.pallas import tpu as pltpu
from jax.sharding import PartitionSpec as P

KERNEL = 7
STRIDE = 8
UNITS = 3
DILATIONS = (1, 3, 9)
LANES = 128
LEFT = 48
SENT = 48
HALO = 40
SEGMENTS = 16
SIDE = 3
TABLE = 8
IN_RATE, IN_SCALE, MID_RATE, MID_SCALE, WIDE, POINT = range(6)

SINE = (9.86952481, -32.46513948, 42.64342537, -29.42627071, 10.5812946)


def snake(values, rate, scale):
    turns = values * rate
    rest = turns - jnp.round(turns)
    square = rest * rest
    sine = jnp.float32(SINE[4])
    for coefficient in SINE[3::-1]:
        sine = sine * square + jnp.float32(coefficient)
    return values + (sine * square) * scale


def rounded(values):
    return values.astype(jnp.bfloat16).astype(jnp.float32)


def lane(c):
    return slice(c * LANES, (c + 1) * LANES)


def entry(table, unit, which, lanes=slice(None)):
    row = unit * TABLE + which
    return table[row : row + 1, lanes]


def gather(s_rows, tiles, at, start, length, count):
    for j in range(count):
        for c in range(s_rows.shape[0]):
            low = s_rows[c, pl.ds(start + j, 8, stride=length), :]
            high = s_rows[c, pl.ds(start + j + 8 * length, 8, stride=length), :]
            row = (at + j) * SEGMENTS
            tiles[row : row + SEGMENTS, lane(c)] = jnp.concatenate([low, high], axis=0).astype(
                jnp.bfloat16
            )


def residual(unit, table, taps, point, windows):
    middle = None
    for k in range(KERNEL):
        product = jnp.dot(windows(k), taps[unit, k], preferred_element_type=jnp.float32)
        middle = product if middle is None else middle + product
    gated = snake(
        middle + entry(table, unit, WIDE),
        entry(table, unit, MID_RATE),
        entry(table, unit, MID_SCALE),
    )
    update = jnp.dot(
        gated.astype(jnp.bfloat16), point[unit], preferred_element_type=jnp.float32
    )
    return update + entry(table, unit, POINT)


def scatter(update, x_rows, out_rows, base, length, begin, end, after=None):
    for c in range(x_rows.shape[0]):
        for j in range(begin, end):
            for half in range(2):
                row = (j - begin) * SEGMENTS + half * 8
                where = pl.ds(base + j + half * 8 * length, 8, stride=length)
                current = rounded(x_rows[c, where, :] + update[row : row + 8, lane(c)])
                out_rows[c, where, :] = current
                if after is not None:
                    after(c, where, current)


def halves(length, parts=2):
    cuts = [length * part // parts for part in range(parts + 1)]
    return list(zip(cuts[:-1], cuts[1:]))


def place():
    return lax.axis_index("tm")


def edges_kernel(up_hbm, *refs):
    params, (x_own, to_far, to_near, table), (up, held, sems) = refs[:6], refs[6:10], refs[10:]
    frames = up.shape[1]
    copies = [pltpu.make_async_copy(up_hbm, up, sems.at[6])]
    for i, param in enumerate(params):
        copies.append(pltpu.make_async_copy(param, held.at[i], sems.at[i]))
    for copy in copies:
        copy.start()
    for copy in copies:
        copy.wait()
    later = up[1].astype(jnp.float32)
    none = jnp.zeros((STRIDE, later.shape[1]), jnp.float32)
    later = jnp.concatenate([none, later], axis=0)
    own = up[0].astype(jnp.float32)
    x_own[...] = (own + later[:frames]).astype(jnp.bfloat16)
    to_next = jnp.concatenate([own[frames - HALO :], none], axis=0) + later[frames - HALO :]
    to_last = own[:SENT] + later[:SENT]
    odd = place() % 2 == 1
    to_far[...] = jnp.where(odd, to_next, to_last).astype(jnp.bfloat16)
    to_near[...] = jnp.where(odd, to_last, to_next).astype(jnp.bfloat16)
    table[UNITS * TABLE :, :] = later[frames:]
    wide, point, alpha_in, beta_in, alpha_mid, beta_mid = (held[i] for i in range(6))
    rows = (alpha_in / math.pi, 1 / beta_in, alpha_mid / math.pi, 1 / beta_mid, wide, point)
    for which, value in enumerate(rows):
        for unit in range(UNITS):
            row = unit * TABLE + which
            table[row : row + 1, :] = value[unit : unit + 1, :]


def inner_plan(frames):
    return STRIDE, (frames - 2 * STRIDE) // SEGMENTS


def inner_kernel(x_own, table, taps, point, x_next, x_rows, s_rows, tiles):
    frames = x_own.shape[0]
    groups = x_rows.shape[0]
    first, length = inner_plan(frames)
    for c in range(groups):
        current = x_own[:, lane(c)].astype(jnp.float32)
        x_rows[c, LEFT : LEFT + frames, :] = current
        s_rows[c, LEFT : LEFT + frames, :] = snake(
            current, entry(table, 0, IN_RATE, lane(c)), entry(table, 0, IN_SCALE, lane(c))
        )
    base = LEFT + first
    gather(s_rows, tiles, 0, base - 3, length, length + 6)
    for begin, end in halves(length):
        update = residual(
            0, table, taps, point,
            lambda k: tiles[(begin + k) * SEGMENTS : (end + k) * SEGMENTS, :],
        )
        scatter(update, x_rows, x_next, base, length, begin, end)


def outer_plan(frames):
    plan = {}
    for unit in range(1, UNITS):
        reach = 3 * sum(DILATIONS[unit + 1 :])
        first = -(-reach // 8) * 8
        length = -(-(frames + 2 * first) // SEGMENTS)
        if length % 8 == 0:
            length += 1
        plan[unit] = (-first, length)
    return plan


def outer_kernel(
    tracks,
    x_own, x_inner, from_chip, from_far, table, taps, point,
    out,
    x_rows, s_rows, tiles,
):
    frames = x_own.shape[0]
    groups = x_rows.shape[0]
    end_row = LEFT + frames
    odd = place() % 2 == 1
    is_first = place() == 0
    is_last = place() == tracks - 1

    def snake_in(unit, c, values):
        return snake(
            values, entry(table, unit, IN_RATE, lane(c)), entry(table, unit, IN_SCALE, lane(c))
        )

    def clear_outside(c):
        s_rows[c, 0:LEFT, :] = jnp.where(is_first, 0.0, s_rows[c, 0:LEFT, :])
        s_rows[c, end_row:, :] = jnp.where(is_last, 0.0, s_rows[c, end_row:, :])

    inner_first, inner_length = inner_plan(frames)
    inner_end = LEFT + inner_first + inner_length * SEGMENTS
    low_end = LEFT + 2 * STRIDE
    for c in range(groups):
        chip = from_chip[:, lane(c)].astype(jnp.float32)
        far = from_far[:, lane(c)].astype(jnp.float32)
        before = jnp.where(odd, chip, far)
        behind = jnp.where(odd, far, chip)
        carried = jnp.where(is_first, 0.0, before[HALO:SENT])
        own_low = x_own[: 2 * STRIDE, lane(c)].astype(jnp.float32)
        own_high = x_own[frames - 2 * STRIDE :, lane(c)].astype(jnp.float32)
        low = jnp.concatenate(
            [before[:HALO], rounded(own_low[:STRIDE] + carried), own_low[STRIDE:]], axis=0
        )
        joint = rounded(behind[:STRIDE] + table[UNITS * TABLE :, lane(c)])
        high = jnp.concatenate([own_high, joint, behind[STRIDE:HALO]], axis=0)
        x_rows[c, LEFT - HALO : low_end, :] = low
        x_rows[c, end_row - 2 * STRIDE : end_row + HALO, :] = high
        s_rows[c, LEFT - HALO : low_end, :] = snake_in(0, c, low)
        s_rows[c, end_row - 2 * STRIDE : end_row + HALO, :] = snake_in(0, c, high)
        clear_outside(c)
    bases = (LEFT - 36, inner_end)
    side = SIDE + 6
    for at, base in enumerate(bases):
        gather(s_rows, tiles, at * side, base - 3, SIDE, side)

    def edge_windows(k):
        parts = [(at * side + k) * SEGMENTS for at in range(2)]
        return jnp.concatenate([tiles[p : p + SIDE * SEGMENTS, :] for p in parts], axis=0)

    update = residual(0, table, taps, point, edge_windows)
    for at, base in enumerate(bases):
        part = update[at * SIDE * SEGMENTS : (at + 1) * SIDE * SEGMENTS]
        scatter(part, x_rows, x_rows, base, SIDE, 0, SIDE)
    for c in range(groups):
        tile = slice(low_end - 8, low_end)
        row = lax.broadcasted_iota(jnp.int32, (8, LANES), 0)
        x_rows[c, tile, :] = jnp.where(row < 4, x_rows[c, tile, :], x_inner[c, tile, :])
        x_rows[c, low_end:inner_end, :] = x_inner[c, low_end:inner_end, :]
        rows = slice(LEFT - HALO, end_row + HALO)
        s_rows[c, rows, :] = snake_in(1, c, x_rows[c, rows, :])
        clear_outside(c)

    for unit, (first, length) in outer_plan(frames).items():
        dilation = DILATIONS[unit]
        base = LEFT + first
        gather(s_rows, tiles, 0, base - 3 * dilation, length, length + 6 * dilation)

        def after(c, where, current):
            s_rows[c, where, :] = snake_in(unit + 1, c, current)

        for begin, end in halves(length):
            update = residual(
                unit, table, taps, point,
                lambda k: tiles[
                    (begin + k * dilation) * SEGMENTS : (end + k * dilation) * SEGMENTS, :
                ],
            )
            scatter(
                update, x_rows, x_rows, base, length, begin, end,
                after if unit + 1 < UNITS else None,
            )
        if unit + 1 < UNITS:
            for c in range(groups):
                clear_outside(c)

    for c in range(groups):
        out[:, lane(c)] = x_rows[c, LEFT:end_row, :].astype(jnp.bfloat16)


def swaps(groups, count):
    near, far = [], []
    for group in range(groups):
        for index in range(count):
            me = group * count + index
            near.append((me, group * count + (index ^ 1)))
            if index == 0 or index == count - 1:
                far.append((me, (group ^ 1) * count + index))
            else:
                far.append((me, me + 1 if index % 2 else me - 1))
    return near, far


VMEM = pl.BlockSpec(memory_space=pltpu.VMEM)
HBM = pl.BlockSpec(memory_space=pltpu.HBM)


def in_hbm(value):
    return pltpu.with_memory_space_constraint(value, pltpu.HBM)


def per_device(
    upsampled, taps, bias_wide, pointwise, bias_point, alpha_in, beta_in, alpha_mid, beta_mid
):
    frames, channels = upsampled.shape[1:]
    count = lax.axis_size("tm")
    near, far = swaps(lax.axis_size("grp"), count)
    groups = channels // LANES
    rows = frames + 2 * LEFT
    half = jnp.bfloat16
    params = (bias_wide, bias_point, alpha_in, beta_in, alpha_mid, beta_mid)
    limit = pltpu.CompilerParams(vmem_limit_bytes=16 * 2**20)

    x_own, to_far, to_near, table = pl.pallas_call(
        edges_kernel,
        out_shape=(
            jax.ShapeDtypeStruct((frames, channels), half),
            jax.ShapeDtypeStruct((SENT, channels), half),
            jax.ShapeDtypeStruct((SENT, channels), half),
            jax.ShapeDtypeStruct((UNITS * TABLE + STRIDE, channels), jnp.float32),
        ),
        in_specs=[HBM] * 7,
        out_specs=(VMEM,) * 4,
        scratch_shapes=[
            pltpu.VMEM(upsampled.shape, half),
            pltpu.VMEM((6,) + bias_wide.shape, jnp.float32),
            pltpu.SemaphoreType.DMA((7,)),
        ],
        compiler_params=limit,
        cost_estimate=pl.CostEstimate(
            flops=6 * 10**9, bytes_accessed=upsampled.size * 2, transcendentals=0
        ),
        name="edges",
    )(in_hbm(upsampled), *(in_hbm(param) for param in params))

    from_far = lax.ppermute(to_far, ("grp", "tm"), far)
    from_chip = lax.ppermute(to_near, ("grp", "tm"), near)

    held = pltpu.VMEM((groups, rows, LANES), jnp.float32)
    inner_length = inner_plan(frames)[1]
    x_inner = pl.pallas_call(
        inner_kernel,
        out_shape=jax.ShapeDtypeStruct((groups, rows, LANES), jnp.float32),
        in_specs=[VMEM] * 4,
        out_specs=VMEM,
        scratch_shapes=[
            held,
            held,
            pltpu.VMEM(((inner_length + 6) * SEGMENTS, channels), half),
        ],
        compiler_params=limit,
        cost_estimate=pl.CostEstimate(
            flops=2 * (KERNEL + 1) * inner_length * SEGMENTS * channels**2,
            bytes_accessed=taps.size * 2,
            transcendentals=0,
        ),
        name="inner",
    )(x_own, table, taps, pointwise)

    reach = max(
        length + 6 * DILATIONS[unit] for unit, (_, length) in outer_plan(frames).items()
    )
    return pl.pallas_call(
        functools.partial(outer_kernel, count),
        out_shape=jax.ShapeDtypeStruct((frames, channels), half),
        in_specs=[VMEM] * 7,
        out_specs=VMEM,
        scratch_shapes=[held, held, pltpu.VMEM((reach * SEGMENTS, channels), half)],
        compiler_params=limit,
        name="outer",
    )(x_own, x_inner, from_chip, from_far, table, taps, pointwise)


def solution(mesh):
    placed = (P(None, ("grp", "tm"), None), P(), P(), P(), P(), P(), P(), P(), P())
    return jax.shard_map(
        per_device, mesh=mesh, in_specs=placed, out_specs=P(("grp", "tm"), None), check_vma=False
    )
```

```python
import functools
import math

import jax
import jax.numpy as jnp
from jax import lax
from jax.experimental import pallas as pl
from jax.experimental.pallas import tpu as pltpu
from jax.sharding import PartitionSpec as P

KERNEL = 7
STRIDE = 8
UNITS = 3
DILATIONS = (1, 3, 9)
LANES = 128
LEFT = 48
SENT = 48
HALO = 40
SEGMENTS = 16
TABLE = 8
IN_RATE, IN_SCALE, MID_RATE, MID_SCALE, WIDE, POINT = range(6)

SINE = (9.86952481, -32.46513948, 42.64342537, -29.42627071, 10.5812946)


def snake(values, rate, scale):
    turns = values * rate
    rest = turns - jnp.round(turns)
    square = rest * rest
    sine = jnp.float32(SINE[4])
    for coefficient in SINE[3::-1]:
        sine = sine * square + jnp.float32(coefficient)
    return values + (sine * square) * scale


def rounded(values):
    return values.astype(jnp.bfloat16).astype(jnp.float32)


def lane(c):
    return slice(c * LANES, (c + 1) * LANES)


def entry(table, unit, which, lanes=slice(None)):
    row = unit * TABLE + which
    return table[row : row + 1, lanes]


class Part:
    def __init__(self, unit, pieces):
        self.unit = unit
        self.dilation = DILATIONS[unit]
        self.pieces = pieces
        self.rows = SEGMENTS * sum(length for _, length in pieces)
        self.tiles = sum(length + 6 * self.dilation for _, length in pieces)

    def gather(self, s_rows, tiles):
        steps = []

        def step(at, start, length):
            rows = slice(at * SEGMENTS, (at + 1) * SEGMENTS)
            for c in range(s_rows.shape[0]):
                low = s_rows[c, pl.ds(start, 8, stride=length), :]
                high = s_rows[c, pl.ds(start + 8 * length, 8, stride=length), :]
                tiles[rows, lane(c)] = jnp.concatenate([low, high], axis=0).astype(jnp.bfloat16)

        for first, length in self.pieces:
            start = LEFT + first - 3 * self.dilation
            for j in range(length + 6 * self.dilation):
                steps.append((10, functools.partial(step, len(steps), start + j, length)))
        return steps

    def window(self, tiles, k):
        at, found = 0, []
        for _, length in self.pieces:
            row = (at + k * self.dilation) * SEGMENTS
            found.append(tiles[row : row + length * SEGMENTS, :])
            at += length + 6 * self.dilation
        return found[0] if len(found) == 1 else jnp.concatenate(found, axis=0)

    def conv(self, tiles, taps, middle):
        channels = middle.shape[1]
        total = [None]

        def step(columns, k):
            product = jnp.dot(
                self.window(tiles, k),
                taps[self.unit, k, :, columns],
                preferred_element_type=jnp.float32,
            )
            total[0] = product if k == 0 else total[0] + product
            if k == KERNEL - 1:
                middle[: self.rows, columns] = total[0]

        return [
            (1, functools.partial(step, columns, k))
            for columns in halves(channels)
            for k in range(KERNEL)
        ]

    def gate(self, middle, gated, table, columns=slice(None)):
        def step(rows):
            gated[rows, columns] = snake(
                middle[rows, columns] + entry(table, self.unit, WIDE, columns),
                entry(table, self.unit, MID_RATE, columns),
                entry(table, self.unit, MID_SCALE, columns),
            ).astype(jnp.bfloat16)

        return [
            (40, functools.partial(step, slice(row, row + SEGMENTS)))
            for row in range(0, self.rows, SEGMENTS)
        ]

    def project(self, sources, point, update):
        total = [None]

        def step(i, gated, columns):
            product = jnp.dot(
                gated[: self.rows, columns],
                point[self.unit, columns, :],
                preferred_element_type=jnp.float32,
            )
            total[0] = product if i == 0 else total[0] + product
            if i == len(sources) - 1:
                update[: self.rows, :] = total[0]

        return [
            (20, functools.partial(step, i, gated, columns))
            for i, (gated, columns) in enumerate(sources)
        ]

    def finish(self, update, table, x_rows, x_next, s_next=None):
        steps = []

        def step(row, start, length):
            for half in range(2):
                where = pl.ds(start + half * 8 * length, 8, stride=length)
                rows = slice(row + half * 8, row + half * 8 + 8)
                for c in range(x_rows.shape[0]):
                    change = update[rows, lane(c)] + entry(table, self.unit, POINT, lane(c))
                    current = rounded(x_rows[c, where, :] + change)
                    x_next[c, where, :] = current
                    if s_next is not None:
                        s_next[c, where, :] = snake_in(table, self.unit + 1, c, current)

        for first, length in self.pieces:
            for j in range(length):
                steps.append(
                    (50, functools.partial(step, len(steps) * SEGMENTS, LEFT + first + j, length))
                )
        return steps


def snake_in(table, unit, c, values):
    return snake(
        values, entry(table, unit, IN_RATE, lane(c)), entry(table, unit, IN_SCALE, lane(c))
    )


def weave(main, others=()):
    whole = sum(cost for cost, _ in others)
    spent, at = 0, 0
    for i, (_, step) in enumerate(main):
        step()
        while at < len(others) and (i + 1 == len(main) or spent * len(main) < whole * (i + 1)):
            spent += others[at][0]
            others[at][1]()
            at += 1


def run(steps):
    for _, step in steps:
        step()


def halves(channels):
    return slice(0, channels // 2), slice(channels // 2, channels)


def parts(frames):
    inner = (
        Part(0, [(8, frames // SEGMENTS - 6)]),
        Part(1, [(20, frames // SEGMENTS - 7)]),
        Part(2, [(48, frames // SEGMENTS - 11)]),
    )
    outer = (
        Part(0, [(-36, 3), (frames - 88, 8)]),
        Part(1, [(-28, 3), (frames - 100, 8)]),
        Part(2, [(0, 3), (frames - 128, 8)]),
    )
    return inner, outer


def place():
    return lax.axis_index("tm")


def edges_kernel(up_hbm, *refs):
    params, (x_own, to_far, to_near, table), (up, held, sems) = refs[:6], refs[6:10], refs[10:]
    frames = up.shape[1]
    copies = [pltpu.make_async_copy(up_hbm, up, sems.at[6])]
    for i, param in enumerate(params):
        copies.append(pltpu.make_async_copy(param, held.at[i], sems.at[i]))
    for copy in copies:
        copy.start()
    for copy in copies:
        copy.wait()
    later = up[1].astype(jnp.float32)
    none = jnp.zeros((STRIDE, later.shape[1]), jnp.float32)
    later = jnp.concatenate([none, later], axis=0)
    own = up[0].astype(jnp.float32)
    x_own[...] = (own + later[:frames]).astype(jnp.bfloat16)
    to_next = jnp.concatenate([own[frames - HALO :], none], axis=0) + later[frames - HALO :]
    to_last = own[:SENT] + later[:SENT]
    odd = place() % 2 == 1
    to_far[...] = jnp.where(odd, to_next, to_last).astype(jnp.bfloat16)
    to_near[...] = jnp.where(odd, to_last, to_next).astype(jnp.bfloat16)
    table[UNITS * TABLE :, :] = later[frames:]
    wide, point, alpha_in, beta_in, alpha_mid, beta_mid = (held[i] for i in range(6))
    rows = (alpha_in / math.pi, 1 / beta_in, alpha_mid / math.pi, 1 / beta_mid, wide, point)
    for which, value in enumerate(rows):
        for unit in range(UNITS):
            row = unit * TABLE + which
            table[row : row + 1, :] = value[unit : unit + 1, :]


def first_kernel(x_own, table, x_rows, s_rows, tiles):
    frames = x_own.shape[0]
    for c in range(x_rows.shape[0]):
        current = x_own[:, lane(c)].astype(jnp.float32)
        x_rows[c, LEFT : LEFT + frames, :] = current
        s_rows[c, LEFT : LEFT + frames, :] = snake_in(table, 0, c, current)
    run(parts(frames)[0][0].gather(s_rows, tiles))


def inner_kernel(frames, tiles, table, taps, middle, gated):
    part = parts(frames)[0][0]
    first, _ = halves(middle.shape[1])
    steps = part.conv(tiles, taps, middle)
    weave(steps[:KERNEL])
    weave(steps[KERNEL:], part.gate(middle, gated, table, first))


def outer_kernel(
    tracks,
    x_own, x_first, s_first, first_middle, first_gated, from_chip, from_far, table, taps, point,
    out,
    x_0, x_1, x_2, s_0, s_1, s_2, inner_tiles, outer_tiles, inner_middle, outer_middle,
    gated, gated_2, update,
):
    frames, channels = x_own.shape
    groups = x_0.shape[0]
    end_row = LEFT + frames
    odd = place() % 2 == 1
    is_first = place() == 0
    is_last = place() == tracks - 1
    inner, outer = parts(frames)
    both = halves(channels)

    def clear_outside(s_rows):
        def step(c):
            s_rows[c, 0:LEFT, :] = jnp.where(is_first, 0.0, s_rows[c, 0:LEFT, :])
            s_rows[c, end_row:, :] = jnp.where(is_last, 0.0, s_rows[c, end_row:, :])

        return [(10, functools.partial(step, c)) for c in range(groups)]

    def store(begin, end):
        def step(c, row):
            rows = slice(LEFT + row, LEFT + row + SEGMENTS)
            out[row : row + SEGMENTS, lane(c)] = x_0[c, rows, :].astype(jnp.bfloat16)

        return [
            (2, functools.partial(step, c, row))
            for row in range(begin, end, SEGMENTS)
            for c in range(groups)
        ]

    def after(part, middle, x_rows, x_next, s_next):
        return (
            part.gate(middle, gated, table)
            + part.project([(gated, slice(None))], point, update)
            + part.finish(update, table, x_rows, x_next, s_next)
        )

    low_end = LEFT + 2 * STRIDE
    kept = LEFT + outer[0].pieces[1][0] - 8
    for c in range(groups):
        chip = from_chip[:, lane(c)].astype(jnp.float32)
        far = from_far[:, lane(c)].astype(jnp.float32)
        before = jnp.where(odd, chip, far)
        behind = jnp.where(odd, far, chip)
        carried = jnp.where(is_first, 0.0, before[HALO:SENT])
        own_low = x_own[: 2 * STRIDE, lane(c)].astype(jnp.float32)
        low = jnp.concatenate(
            [before[:HALO], rounded(own_low[:STRIDE] + carried), own_low[STRIDE:]], axis=0
        )
        joint = rounded(behind[:STRIDE] + table[UNITS * TABLE :, lane(c)])
        high = jnp.concatenate([joint, behind[STRIDE:HALO]], axis=0)
        x_0[c, LEFT - HALO : low_end, :] = low
        s_0[c, LEFT - HALO : low_end, :] = snake_in(table, 0, c, low)
        x_0[c, kept:end_row, :] = x_first[c, kept:end_row, :]
        s_0[c, kept:end_row, :] = s_first[c, kept:end_row, :]
        x_0[c, end_row : end_row + HALO, :] = high
        s_0[c, end_row : end_row + HALO, :] = snake_in(table, 0, c, high)
    run(clear_outside(s_0))
    run(outer[0].gather(s_0, outer_tiles))

    weave(
        outer[0].conv(outer_tiles, taps, outer_middle),
        inner[0].gate(first_middle, gated, table, both[1])
        + inner[0].project([(first_gated, both[0]), (gated, both[1])], point, update)
        + inner[0].finish(update, table, x_first, x_1, s_1)
        + inner[1].gather(s_1, inner_tiles),
    )
    weave(
        inner[1].conv(inner_tiles, taps, inner_middle),
        after(outer[0], outer_middle, x_0, x_1, s_1)
        + clear_outside(s_1)
        + outer[1].gather(s_1, outer_tiles),
    )
    weave(
        outer[1].conv(outer_tiles, taps, outer_middle),
        after(inner[1], inner_middle, x_1, x_2, s_2) + inner[2].gather(s_2, inner_tiles),
    )
    weave(
        inner[2].conv(inner_tiles, taps, inner_middle),
        after(outer[1], outer_middle, x_1, x_2, s_2)
        + clear_outside(s_2)
        + outer[2].gather(s_2, outer_tiles),
    )
    begin = inner[2].pieces[0][0]
    end = begin + inner[2].rows
    steps = outer[2].conv(outer_tiles, taps, outer_middle)
    finish = after(inner[2], inner_middle, x_2, x_0, None) + store(begin, end)
    cut = len(finish) // 2
    weave(steps[:KERNEL], finish[:cut])
    weave(steps[KERNEL:], finish[cut:] + outer[2].gate(outer_middle, gated_2, table, both[0]))
    run(outer[2].gate(outer_middle, gated_2, table, both[1]))
    run(outer[2].project([(gated_2, columns) for columns in both], point, update))
    run(outer[2].finish(update, table, x_2, x_0))
    run(store(0, begin) + store(end, frames))


def swaps(groups, count):
    near, far = [], []
    for group in range(groups):
        for index in range(count):
            me = group * count + index
            near.append((me, group * count + (index ^ 1)))
            if index == 0 or index == count - 1:
                far.append((me, (group ^ 1) * count + index))
            else:
                far.append((me, me + 1 if index % 2 else me - 1))
    return near, far


VMEM = pl.BlockSpec(memory_space=pltpu.VMEM)
HBM = pl.BlockSpec(memory_space=pltpu.HBM)


def in_hbm(value):
    return pltpu.with_memory_space_constraint(value, pltpu.HBM)


VMEM = pl.BlockSpec(memory_space=pltpu.VMEM)
HBM = pl.BlockSpec(memory_space=pltpu.HBM)


def in_hbm(value):
    return pltpu.with_memory_space_constraint(value, pltpu.HBM)


def per_device(
    upsampled, taps, bias_wide, pointwise, bias_point, alpha_in, beta_in, alpha_mid, beta_mid
):
    frames, channels = upsampled.shape[1:]
    count = lax.axis_size("tm")
    near, far = swaps(lax.axis_size("grp"), count)
    groups = channels // LANES
    rows = frames + 2 * LEFT
    half = jnp.bfloat16
    params = (bias_wide, bias_point, alpha_in, beta_in, alpha_mid, beta_mid)
    limit = pltpu.CompilerParams(vmem_limit_bytes=16 * 2**20)

    x_own, to_far, to_near, table = pl.pallas_call(
        edges_kernel,
        out_shape=(
            jax.ShapeDtypeStruct((frames, channels), half),
            jax.ShapeDtypeStruct((SENT, channels), half),
            jax.ShapeDtypeStruct((SENT, channels), half),
            jax.ShapeDtypeStruct((UNITS * TABLE + STRIDE, channels), jnp.float32),
        ),
        in_specs=[HBM] * 7,
        out_specs=(VMEM,) * 4,
        scratch_shapes=[
            pltpu.VMEM(upsampled.shape, half),
            pltpu.VMEM((6,) + bias_wide.shape, jnp.float32),
            pltpu.SemaphoreType.DMA((7,)),
        ],
        compiler_params=limit,
        cost_estimate=pl.CostEstimate(
            flops=6 * 10**9, bytes_accessed=upsampled.size * 2, transcendentals=0
        ),
        name="edges",
    )(in_hbm(upsampled), *(in_hbm(param) for param in params))

    from_far = lax.ppermute(to_far, ("grp", "tm"), far)
    from_chip = lax.ppermute(to_near, ("grp", "tm"), near)

    inner, outer = parts(frames)
    natural = (groups, rows, LANES)
    single = jnp.float32

    def tiles(*of):
        return max(part.tiles for part in of) * SEGMENTS, channels

    def most(*of):
        return max(part.rows for part in of), channels

    x_first, s_first, first_tiles = pl.pallas_call(
        first_kernel,
        out_shape=(
            jax.ShapeDtypeStruct(natural, single),
            jax.ShapeDtypeStruct(natural, single),
            jax.ShapeDtypeStruct(tiles(inner[0]), half),
        ),
        in_specs=[VMEM] * 2,
        out_specs=(VMEM,) * 3,
        compiler_params=limit,
        name="first",
    )(x_own, table)

    first_middle, first_gated = pl.pallas_call(
        functools.partial(inner_kernel, frames),
        out_shape=(
            jax.ShapeDtypeStruct(most(inner[0]), single),
            jax.ShapeDtypeStruct(most(inner[0]), half),
        ),
        in_specs=[VMEM] * 3,
        out_specs=(VMEM,) * 2,
        compiler_params=limit,
        cost_estimate=pl.CostEstimate(
            flops=2 * KERNEL * inner[0].rows * channels**2,
            bytes_accessed=taps.size * 2,
            transcendentals=0,
        ),
        name="inner",
    )(first_tiles, table, taps)

    return pl.pallas_call(
        functools.partial(outer_kernel, count),
        out_shape=jax.ShapeDtypeStruct((frames, channels), half),
        in_specs=[VMEM] * 10,
        out_specs=VMEM,
        scratch_shapes=[pltpu.VMEM(natural, single)] * 6
        + [
            pltpu.VMEM(tiles(*inner[1:]), half),
            pltpu.VMEM(tiles(*outer), half),
            pltpu.VMEM(most(*inner[1:]), single),
            pltpu.VMEM(most(*outer), single),
            pltpu.VMEM(most(*inner, *outer), half),
            pltpu.VMEM(most(outer[2]), half),
            pltpu.VMEM(most(*inner, *outer), single),
        ],
        compiler_params=pltpu.CompilerParams(vmem_limit_bytes=24 * 2**20),
        name="outer",
    )(
        x_own, x_first, s_first, first_middle, first_gated, from_chip, from_far,
        table, taps, pointwise,
    )


def solution(mesh):
    placed = (P(None, ("grp", "tm"), None), P(), P(), P(), P(), P(), P(), P(), P())
    return jax.shard_map(
        per_device, mesh=mesh, in_specs=placed, out_specs=P(("grp", "tm"), None), check_vma=False
    )
```

```python
import functools
import math

import jax
import jax.numpy as jnp
from jax import lax
from jax.experimental import pallas as pl
from jax.experimental.pallas import tpu as pltpu
from jax.sharding import PartitionSpec as P

KERNEL = 7
STRIDE = 8
UNITS = 3
DILATIONS = (1, 3, 9)
LANES = 128
LEFT = 48
SENT = 48
HALO = 40
SEGMENTS = 16
TABLE = 8
IN_RATE, IN_SCALE, MID_RATE, MID_SCALE, WIDE, POINT = range(6)

SINE = (9.86952481, -32.46513948, 42.64342537, -29.42627071, 10.5812946)


def snake(values, rate, scale):
    turns = values * rate
    rest = turns - jnp.round(turns)
    square = rest * rest
    sine = jnp.float32(SINE[4])
    for coefficient in SINE[3::-1]:
        sine = sine * square + jnp.float32(coefficient)
    return values + (sine * square) * scale


def rounded(values):
    return values.astype(jnp.bfloat16).astype(jnp.float32)


def lane(c):
    return slice(c * LANES, (c + 1) * LANES)


def entry(table, unit, which, lanes=slice(None)):
    row = unit * TABLE + which
    return table[row : row + 1, lanes]


WIDTH = 256


class Matrix:
    def __init__(self):
        self.count = 0
        self.staged = None

    def tile(self, weights, rows, sums):
        register = self.count % 2
        self.count += 1
        for unit, columns in enumerate(halves(2 * WIDTH)):
            pltpu.matmul_push_rhs(weights(columns), register, unit)
        self.flush()
        self.staged = register, rows, sums

    def flush(self):
        if self.staged is None:
            return
        register, rows, sums = self.staged
        self.staged = None
        for i, pair in enumerate(sums):
            value = rows(i)
            for unit in range(2):
                load = register if i == 0 else None
                pltpu.matmul_acc_lhs(pair[unit], value, load_staged_rhs=load)


class Part:
    def __init__(self, unit, pieces, plain=False):
        self.unit = unit
        self.plain = plain
        self.dilation = DILATIONS[unit]
        self.pieces = pieces
        self.rows = SEGMENTS * sum(length for _, length in pieces)
        if plain:
            self.tiles = KERNEL * self.rows // SEGMENTS
        else:
            self.tiles = sum(length + 6 * self.dilation for _, length in pieces)

    def starts(self, first, j, length):
        if self.plain:
            start = LEFT + first + SEGMENTS * j
            return (start, start + 8), 1
        start = LEFT + first + j
        return (start, start + 8 * length), length

    def gather(self, s_rows, tiles):
        steps = []

        def step(at, first, j, length):
            rows = slice(at * SEGMENTS, (at + 1) * SEGMENTS)
            starts, stride = self.starts(first, j, length)
            for c in range(s_rows.shape[0]):
                both = [s_rows[c, run_of(start, stride), :] for start in starts]
                tiles[rows, lane(c)] = jnp.concatenate(both, axis=0).astype(jnp.bfloat16)

        reach = 3 * self.dilation
        if self.plain:
            for k in range(KERNEL):
                for first, length in self.pieces:
                    first += (k - 3) * self.dilation
                    for j in range(length):
                        steps.append((10, functools.partial(step, len(steps), first, j, length)))
            return steps
        for first, length in self.pieces:
            for j in range(length + 2 * reach):
                steps.append(
                    (10, functools.partial(step, len(steps), first - reach, j, length))
                )
        return steps

    def window(self, tiles, k):
        at, found = 0, []
        for _, length in self.pieces:
            row = (at + k * self.dilation) * SEGMENTS
            found.append(tiles[row : row + length * SEGMENTS, :])
            at += length + 6 * self.dilation
        return found[0] if len(found) == 1 else jnp.concatenate(found, axis=0)

    def conv(self, tiles, taps, middle):
        channels = middle.shape[1]
        total = [None]

        def step(columns, k):
            product = jnp.dot(
                self.window(tiles, k),
                taps[self.unit, k, :, columns],
                preferred_element_type=jnp.float32,
            )
            total[0] = product if k == 0 else total[0] + product
            if k == KERNEL - 1:
                middle[: self.rows, columns] = total[0]

        return [
            (1, functools.partial(step, columns, k))
            for columns in halves(channels)
            for k in range(KERNEL)
        ]

    def conv_sums(self, matrix, tiles, taps, sums):
        places, at = [], 0
        for _, length in self.pieces:
            places += range(at, at + length)
            at += length + (0 if self.plain else 6 * self.dilation)
        away = len(places) if self.plain else self.dilation

        def rows(k, inputs, i):
            row = (places[i] + k * away) * SEGMENTS
            return tiles[row : row + SEGMENTS, inputs]

        def step(k, inputs):
            matrix.tile(
                lambda columns: taps[self.unit, k, inputs, columns],
                functools.partial(rows, k, inputs),
                sums[: len(places)],
            )

        steps = [
            (1, functools.partial(step, k, inputs))
            for k in range(KERNEL)
            for inputs in halves(taps.shape[2])
        ]
        return steps + [(1, matrix.flush)]

    def gate_values(self, values, gated, table, columns):
        gated_values = snake(
            values + entry(table, self.unit, WIDE, columns),
            entry(table, self.unit, MID_RATE, columns),
            entry(table, self.unit, MID_SCALE, columns),
        )
        return gated_values.astype(jnp.bfloat16)

    def gate(self, middle, gated, table, columns):
        def step(rows):
            gated[rows, columns] = self.gate_values(middle[rows, columns], gated, table, columns)

        return [
            (20, functools.partial(step, slice(row, row + SEGMENTS)))
            for row in range(0, self.rows, SEGMENTS)
        ]

    def gate_sums(self, sums, gated, table):
        def step(i):
            rows = slice(i * SEGMENTS, (i + 1) * SEGMENTS)
            for unit, columns in enumerate(halves(gated.shape[1])):
                values = pltpu.matmul_pop(sums[i][unit])
                gated[rows, columns] = self.gate_values(values, gated, table, columns)

        return [(40, functools.partial(step, i)) for i in range(self.rows // SEGMENTS)]

    def project(self, matrix, sources, point, sums):
        def rows(gated, columns, i):
            return gated[i * SEGMENTS : (i + 1) * SEGMENTS, columns]

        def step(gated, inputs):
            matrix.tile(
                lambda columns: point[self.unit, inputs, columns],
                functools.partial(rows, gated, inputs),
                sums[: self.rows // SEGMENTS],
            )

        steps = [(5, functools.partial(step, gated, columns)) for gated, columns in sources]
        return steps + [(5, matrix.flush)]

    def finish(self, sums, table, x_rows, x_next, s_next=None):
        steps = []

        def step(i, first, j, length):
            starts, stride = self.starts(first, j, length)
            update = [pltpu.matmul_pop(sums[i][unit]) for unit in range(2)]
            for half in range(2):
                where = run_of(starts[half], stride)
                rows = slice(half * 8, half * 8 + 8)
                for c in range(x_rows.shape[0]):
                    unit, group = divmod(c, WIDTH // LANES)
                    change = update[unit][rows, lane(group)] + entry(
                        table, self.unit, POINT, lane(c)
                    )
                    current = rounded(x_rows[c, where, :] + change)
                    x_next[c, where, :] = current
                    if s_next is not None:
                        s_next[c, where, :] = snake_in(table, self.unit + 1, c, current)

        for first, length in self.pieces:
            for j in range(length):
                cost = 25 if s_next is None else 50
                steps.append(
                    (cost, functools.partial(step, len(steps), first, j, length))
                )
        return steps


def run_of(start, stride):
    return pl.ds(start, 8) if stride == 1 else pl.ds(start, 8, stride=stride)


def snake_in(table, unit, c, values):
    return snake(
        values, entry(table, unit, IN_RATE, lane(c)), entry(table, unit, IN_SCALE, lane(c))
    )


def weave(main, others=()):
    whole = sum(cost for cost, _ in others)
    spent, at = 0, 0
    for i, (_, step) in enumerate(main):
        step()
        while at < len(others) and (i + 1 == len(main) or spent * len(main) < whole * (i + 1)):
            spent += others[at][0]
            others[at][1]()
            at += 1


def run(steps):
    for _, step in steps:
        step()


def halves(channels):
    return slice(0, channels // 2), slice(channels // 2, channels)


def parts(frames):
    inner = (
        Part(0, [(8, frames // SEGMENTS - 6)]),
        Part(1, [(20, frames // SEGMENTS - 7)]),
        Part(2, [(48, frames // SEGMENTS - 11)]),
    )
    outer = (
        Part(0, [(-36, 3), (frames - 88, 8)]),
        Part(1, [(-28, 3), (frames - 100, 8)], plain=True),
        Part(2, [(0, 3), (frames - 128, 8)], plain=True),
    )
    return inner, outer


def place():
    return lax.axis_index("tm")


def edges_kernel(up_hbm, to_far, to_near, held, sems):
    frames = up_hbm.shape[1]
    copies = []
    for part in range(2):
        for end, row in enumerate((0, frames - SENT)):
            copies.append(
                pltpu.make_async_copy(
                    up_hbm.at[part, pl.ds(row, SENT)], held.at[part, end], sems.at[part, end]
                )
            )
    for copy in copies:
        copy.start()
    for copy in copies:
        copy.wait()
    odd = place() % 2 == 1
    for c in range(up_hbm.shape[2] // LANES):
        own_low, own_high = (held[0, end, :, lane(c)].astype(jnp.float32) for end in range(2))
        low, high = (held[1, end, :, lane(c)].astype(jnp.float32) for end in range(2))
        none = jnp.zeros((STRIDE, LANES), jnp.float32)
        to_next = jnp.concatenate([own_high[STRIDE:], none], axis=0) + high
        to_last = own_low + jnp.concatenate([none, low[:HALO]], axis=0)
        to_far[:, lane(c)] = jnp.where(odd, to_next, to_last).astype(jnp.bfloat16)
        to_near[:, lane(c)] = jnp.where(odd, to_last, to_next).astype(jnp.bfloat16)


def first_kernel(
    up, wide, point, alpha_in, beta_in, alpha_mid, beta_mid, x_rows, s_rows, tiles, table
):
    frames = up.shape[1]
    rows = (
        alpha_in[...] / math.pi, 1 / beta_in[...], alpha_mid[...] / math.pi, 1 / beta_mid[...],
        wide[...], point[...],
    )
    for which, value in enumerate(rows):
        for unit in range(UNITS):
            row = unit * TABLE + which
            table[row : row + 1, :] = value[unit : unit + 1, :]
    for c in range(x_rows.shape[0]):
        later = up[1, :, lane(c)].astype(jnp.float32)
        none = jnp.zeros((STRIDE, LANES), jnp.float32)
        own = up[0, :, lane(c)].astype(jnp.float32)
        current = rounded(own + jnp.concatenate([none, later[: frames - STRIDE]], axis=0))
        table[UNITS * TABLE :, lane(c)] = later[frames - STRIDE :]
        x_rows[c, LEFT : LEFT + frames, :] = current
        s_rows[c, LEFT : LEFT + frames, :] = snake_in(table, 0, c, current)
    run(parts(frames)[0][0].gather(s_rows, tiles))


def inner_kernel(frames, tiles, table, taps, middle, gated):
    part = parts(frames)[0][0]
    first, _ = halves(middle.shape[1])
    steps = part.conv(tiles, taps, middle)
    weave(steps[:KERNEL])
    weave(steps[KERNEL:], part.gate(middle, gated, table, first))


def outer_kernel(
    tracks,
    x_first, s_first, first_middle, first_gated, from_chip, from_far, table, taps, point,
    out,
    x_0, x_1, x_2, s_0, s_1, s_2, inner_tiles, outer_tiles, gated,
):
    inner, outer = parts(out.shape[0])

    def sums(*of):
        one = [pltpu.ACC(unit)((SEGMENTS, WIDTH), jnp.float32) for unit in range(2)]
        return [one] * (max(part.rows for part in of) // SEGMENTS)

    def scoped(inner_sums, outer_sums, update_sums):
        outer_body(
            tracks,
            x_first, s_first, first_middle, first_gated, from_chip, from_far, table, taps,
            point, out,
            x_0, x_1, x_2, s_0, s_1, s_2, inner_tiles, outer_tiles, gated,
            inner_sums, outer_sums, update_sums,
        )

    pl.run_scoped(scoped, sums(*inner[1:]), sums(*outer), sums(*inner, *outer))


def outer_body(
    tracks,
    x_first, s_first, first_middle, first_gated, from_chip, from_far, table, taps, point,
    out,
    x_0, x_1, x_2, s_0, s_1, s_2, inner_tiles, outer_tiles, gated,
    inner_sums, outer_sums, update_sums,
):
    frames, channels = out.shape
    groups = x_0.shape[0]
    end_row = LEFT + frames
    odd = place() % 2 == 1
    is_first = place() == 0
    is_last = place() == tracks - 1
    inner, outer = parts(frames)
    both = halves(channels)

    def clear_outside(s_rows):
        def step(c):
            s_rows[c, 0:LEFT, :] = jnp.where(is_first, 0.0, s_rows[c, 0:LEFT, :])
            s_rows[c, end_row:, :] = jnp.where(is_last, 0.0, s_rows[c, end_row:, :])

        return [(10, functools.partial(step, c)) for c in range(groups)]

    def store(begin, end):
        def step(c, row):
            rows = slice(LEFT + row, LEFT + row + SEGMENTS)
            out[row : row + SEGMENTS, lane(c)] = x_0[c, rows, :].astype(jnp.bfloat16)

        return [
            (2, functools.partial(step, c, row))
            for row in range(begin, end, SEGMENTS)
            for c in range(groups)
        ]

    matrix = Matrix()

    def after(part, sums, x_rows, x_next, s_next):
        return (
            part.gate_sums(sums, gated, table)
            + part.project(matrix, [(gated, columns) for columns in both], point, update_sums)
            + part.finish(update_sums, table, x_rows, x_next, s_next)
        )

    low_end = LEFT + 2 * STRIDE
    kept = LEFT + outer[0].pieces[1][0] - 8
    for c in range(groups):
        chip = from_chip[:, lane(c)].astype(jnp.float32)
        far = from_far[:, lane(c)].astype(jnp.float32)
        before = jnp.where(odd, chip, far)
        behind = jnp.where(odd, far, chip)
        carried = jnp.where(is_first, 0.0, before[HALO:SENT])
        own_low = x_first[c, LEFT:low_end, :]
        low = jnp.concatenate(
            [before[:HALO], rounded(own_low[:STRIDE] + carried), own_low[STRIDE:]], axis=0
        )
        joint = rounded(behind[:STRIDE] + table[UNITS * TABLE :, lane(c)])
        high = jnp.concatenate([joint, behind[STRIDE:HALO]], axis=0)
        x_0[c, LEFT - HALO : low_end, :] = low
        s_0[c, LEFT - HALO : low_end, :] = snake_in(table, 0, c, low)
        x_0[c, kept:end_row, :] = x_first[c, kept:end_row, :]
        s_0[c, kept:end_row, :] = s_first[c, kept:end_row, :]
        x_0[c, end_row : end_row + HALO, :] = high
        s_0[c, end_row : end_row + HALO, :] = snake_in(table, 0, c, high)
    run(clear_outside(s_0))
    run(outer[0].gather(s_0, outer_tiles))

    weave(
        outer[0].conv_sums(matrix, outer_tiles, taps, outer_sums),
        inner[0].gate(first_middle, gated, table, both[1])
        + inner[0].project(
            matrix, [(first_gated, both[0]), (gated, both[1])], point, update_sums
        )
        + inner[0].finish(update_sums, table, x_first, x_1, s_1)
        + inner[1].gather(s_1, inner_tiles),
    )
    weave(
        inner[1].conv_sums(matrix, inner_tiles, taps, inner_sums),
        after(outer[0], outer_sums, x_0, x_1, s_1)
        + clear_outside(s_1)
        + outer[1].gather(s_1, outer_tiles),
    )
    weave(
        outer[1].conv_sums(matrix, outer_tiles, taps, outer_sums),
        after(inner[1], inner_sums, x_1, x_2, s_2) + inner[2].gather(s_2, inner_tiles),
    )
    weave(
        inner[2].conv_sums(matrix, inner_tiles, taps, inner_sums),
        after(outer[1], outer_sums, x_1, x_2, s_2)
        + clear_outside(s_2)
        + outer[2].gather(s_2, outer_tiles),
    )
    begin = inner[2].pieces[0][0]
    end = begin + inner[2].rows
    weave(
        outer[2].conv_sums(matrix, outer_tiles, taps, outer_sums),
        after(inner[2], inner_sums, x_2, x_0, None) + store(begin, end),
    )
    run(after(outer[2], outer_sums, x_2, x_0, None))
    run(store(0, begin) + store(end, frames))


def swaps(groups, count):
    near, far = [], []
    for group in range(groups):
        for index in range(count):
            me = group * count + index
            near.append((me, group * count + (index ^ 1)))
            if index == 0 or index == count - 1:
                far.append((me, (group ^ 1) * count + index))
            else:
                far.append((me, me + 1 if index % 2 else me - 1))
    return near, far


VMEM = pl.BlockSpec(memory_space=pltpu.VMEM)
HBM = pl.BlockSpec(memory_space=pltpu.HBM)


def in_hbm(value):
    return pltpu.with_memory_space_constraint(value, pltpu.HBM)


VMEM = pl.BlockSpec(memory_space=pltpu.VMEM)
HBM = pl.BlockSpec(memory_space=pltpu.HBM)


def in_hbm(value):
    return pltpu.with_memory_space_constraint(value, pltpu.HBM)


def per_device(
    upsampled, taps, bias_wide, pointwise, bias_point, alpha_in, beta_in, alpha_mid, beta_mid
):
    frames, channels = upsampled.shape[1:]
    count = lax.axis_size("tm")
    near, far = swaps(lax.axis_size("grp"), count)
    groups = channels // LANES
    rows = frames + 2 * LEFT
    half = jnp.bfloat16
    params = (bias_wide, bias_point, alpha_in, beta_in, alpha_mid, beta_mid)
    limit = pltpu.CompilerParams(vmem_limit_bytes=16 * 2**20)

    sent = jax.ShapeDtypeStruct((SENT, channels), half)
    to_far, to_near = pl.pallas_call(
        edges_kernel,
        out_shape=(sent, sent),
        in_specs=[HBM],
        out_specs=(VMEM,) * 2,
        scratch_shapes=[
            pltpu.VMEM((2, 2, SENT, channels), half),
            pltpu.SemaphoreType.DMA((2, 2)),
        ],
        compiler_params=limit,
        cost_estimate=pl.CostEstimate(
            flops=6 * 10**9, bytes_accessed=upsampled.size * 2, transcendentals=0
        ),
        name="edges",
    )(in_hbm(upsampled))

    from_far = lax.ppermute(to_far, ("grp", "tm"), far)
    from_chip = lax.ppermute(to_near, ("grp", "tm"), near)

    inner, outer = parts(frames)
    natural = (groups, rows, LANES)
    single = jnp.float32

    def tiles(*of):
        return max(part.tiles for part in of) * SEGMENTS, channels

    def most(*of):
        return max(part.rows for part in of), channels

    x_first, s_first, first_tiles, table = pl.pallas_call(
        first_kernel,
        out_shape=(
            jax.ShapeDtypeStruct(natural, single),
            jax.ShapeDtypeStruct(natural, single),
            jax.ShapeDtypeStruct(tiles(inner[0]), half),
            jax.ShapeDtypeStruct((UNITS * TABLE + STRIDE, channels), single),
        ),
        in_specs=[VMEM] * 7,
        out_specs=(VMEM,) * 4,
        compiler_params=limit,
        name="first",
    )(upsampled, *params)

    first_middle, first_gated = pl.pallas_call(
        functools.partial(inner_kernel, frames),
        out_shape=(
            jax.ShapeDtypeStruct(most(inner[0]), single),
            jax.ShapeDtypeStruct(most(inner[0]), half),
        ),
        in_specs=[VMEM] * 3,
        out_specs=(VMEM,) * 2,
        compiler_params=limit,
        cost_estimate=pl.CostEstimate(
            flops=2 * KERNEL * inner[0].rows * channels**2,
            bytes_accessed=taps.size * 2,
            transcendentals=0,
        ),
        name="inner",
    )(first_tiles, table, taps)

    return pl.pallas_call(
        functools.partial(outer_kernel, count),
        out_shape=jax.ShapeDtypeStruct((frames, channels), half),
        in_specs=[VMEM] * 9,
        out_specs=VMEM,
        scratch_shapes=[pltpu.VMEM(natural, single)] * 6
        + [
            pltpu.VMEM(tiles(*inner[1:]), half),
            pltpu.VMEM(tiles(*outer), half),
            pltpu.VMEM(most(*inner, *outer), half),
        ],
        compiler_params=pltpu.CompilerParams(vmem_limit_bytes=24 * 2**20),
        name="outer",
    )(
        x_first, s_first, first_middle, first_gated, from_chip, from_far,
        table, taps, pointwise,
    )


def solution(mesh):
    placed = (P(None, ("grp", "tm"), None), P(), P(), P(), P(), P(), P(), P(), P())
    return jax.shard_map(
        per_device, mesh=mesh, in_specs=placed, out_specs=P(("grp", "tm"), None), check_vma=False
    )
```

```python
import functools
import math

import jax
import jax.numpy as jnp
from jax import lax
from jax.experimental import pallas as pl
from jax.experimental.pallas import tpu as pltpu
from jax.sharding import PartitionSpec as P

KERNEL = 7
STRIDE = 8
UNITS = 3
DILATIONS = (1, 3, 9)
LANES = 128
LEFT = 48
SENT = 48
HALO = 40
SEGMENTS = 16
TABLE = 16
IN, MID, WIDE, POINT = 0, 5, 10, 11

SINE = (3.141582022, -5.167142795, 2.541899018, -0.5546361724)


def snake(values, rates):
    turns = values * rates[0]
    rest = turns - jnp.round(turns)
    square = rest * rest
    sine = rates[-1]
    for coefficient in rates[-2:0:-1]:
        sine = sine * square + coefficient
    sine = sine * rest
    return values + sine * sine


def rounded(values):
    return values.astype(jnp.bfloat16).astype(jnp.float32)


def lane(c):
    return slice(c * LANES, (c + 1) * LANES)


def entry(table, unit, which, lanes=slice(None)):
    row = unit * TABLE + which
    return table[row : row + 1, lanes]


WIDTH = 256


def rates(table, unit, which, lanes):
    return [entry(table, unit, which + i, lanes) for i in range(5)]


class Matrix:
    def __init__(self):
        self.count = 0
        self.staged = None

    def tile(self, weights, rows, sums):
        register = self.count % 2
        self.count += 1
        for unit, columns in enumerate(halves(2 * WIDTH)):
            pltpu.matmul_push_rhs(weights(columns), register, unit)
        self.flush()
        self.staged = register, rows, sums

    def flush(self):
        if self.staged is None:
            return
        register, rows, sums = self.staged
        self.staged = None
        for i, pair in enumerate(sums):
            value = rows(i)
            for unit in range(2):
                load = register if i == 0 else None
                pltpu.matmul_acc_lhs(pair[unit], value, load_staged_rhs=load)


class Part:
    def __init__(self, unit, pieces, plain=False):
        self.unit = unit
        self.plain = plain
        self.dilation = DILATIONS[unit]
        self.pieces = pieces
        self.rows = SEGMENTS * sum(length for _, length in pieces)
        if plain:
            self.tiles = KERNEL * self.rows // SEGMENTS
        else:
            self.tiles = sum(length + 6 * self.dilation for _, length in pieces)

    def starts(self, first, j, length):
        if self.plain:
            start = LEFT + first + SEGMENTS * j
            return (start, start + 8), 1
        start = LEFT + first + j
        return (start, start + 8 * length), length

    def gather(self, s_rows, tiles):
        steps = [[] for _ in range(KERNEL)]

        def step(at, first, j, length):
            rows = slice(at * SEGMENTS, (at + 1) * SEGMENTS)
            starts, stride = self.starts(first, j, length)
            for c in range(s_rows.shape[0]):
                both = [s_rows[c, run_of(start, stride), :] for start in starts]
                tiles[rows, lane(c)] = jnp.concatenate(both, axis=0).astype(jnp.bfloat16)

        reach = 3 * self.dilation
        for k in range(KERNEL):
            at = 0
            for first, length in self.pieces:
                if self.plain:
                    away = first + (k - 3) * self.dilation
                    new = [(k * self.rows // SEGMENTS + at + j, away, j) for j in range(length)]
                    at += length
                else:
                    begin = length + (k - 1) * self.dilation if k else 0
                    end = length + k * self.dilation
                    new = [(at + j, first - reach, j) for j in range(begin, end)]
                    at += length + 2 * reach
                for tile, start, j in new:
                    steps[k].append((10, functools.partial(step, tile, start, j, length)))
        return steps

    def window(self, tiles, k):
        at, found = 0, []
        for _, length in self.pieces:
            row = (at + k * self.dilation) * SEGMENTS
            found.append(tiles[row : row + length * SEGMENTS, :])
            at += length + 6 * self.dilation
        return found[0] if len(found) == 1 else jnp.concatenate(found, axis=0)

    def conv(self, tiles, taps, middle):
        channels = middle.shape[1]
        total = [None]

        def step(columns, k):
            product = jnp.dot(
                self.window(tiles, k),
                taps[self.unit, k, :, columns],
                preferred_element_type=jnp.float32,
            )
            total[0] = product if k == 0 else total[0] + product
            if k == KERNEL - 1:
                middle[: self.rows, columns] = total[0]

        return [
            (1, functools.partial(step, columns, k))
            for columns in halves(channels)
            for k in range(KERNEL)
        ]

    def conv_sums(self, matrix, tiles, taps, sums):
        places, at = [], 0
        for _, length in self.pieces:
            places += range(at, at + length)
            at += length + (0 if self.plain else 6 * self.dilation)
        away = len(places) if self.plain else self.dilation

        def rows(k, inputs, i):
            row = (places[i] + k * away) * SEGMENTS
            return tiles[row : row + SEGMENTS, inputs]

        def step(k, inputs):
            matrix.tile(
                lambda columns: taps[self.unit, k, inputs, columns],
                functools.partial(rows, k, inputs),
                sums[: len(places)],
            )

        steps = [
            (1, functools.partial(step, k, inputs))
            for k in range(KERNEL)
            for inputs in halves(taps.shape[2])
        ]
        return steps + [(1, matrix.flush)]

    def gate_values(self, values, gated, table, columns):
        gated_values = snake(
            values + entry(table, self.unit, WIDE, columns),
            rates(table, self.unit, MID, columns),
        )
        return gated_values.astype(jnp.bfloat16)

    def gate(self, middle, gated, table, columns):
        def step(rows):
            gated[rows, columns] = self.gate_values(middle[rows, columns], gated, table, columns)

        return [
            (20, functools.partial(step, slice(row, row + SEGMENTS)))
            for row in range(0, self.rows, SEGMENTS)
        ]

    def gate_sums(self, sums, gated, table):
        def step(i):
            rows = slice(i * SEGMENTS, (i + 1) * SEGMENTS)
            for unit, columns in enumerate(halves(gated.shape[1])):
                values = pltpu.matmul_pop(sums[i][unit])
                gated[rows, columns] = self.gate_values(values, gated, table, columns)

        return [(20, functools.partial(step, i)) for i in range(self.rows // SEGMENTS)]

    def project(self, matrix, sources, point, sums):
        def rows(gated, columns, i):
            return gated[i * SEGMENTS : (i + 1) * SEGMENTS, columns]

        def step(gated, inputs):
            matrix.tile(
                lambda columns: point[self.unit, inputs, columns],
                functools.partial(rows, gated, inputs),
                sums[: self.rows // SEGMENTS],
            )

        steps = [(5, functools.partial(step, gated, columns)) for gated, columns in sources]
        return steps + [(5, matrix.flush)]

    def finish(self, sums, table, x_rows, x_next, s_next=None):
        steps = []

        def step(i, first, j, length):
            starts, stride = self.starts(first, j, length)
            update = [pltpu.matmul_pop(sums[i][unit]) for unit in range(2)]
            for half in range(2):
                where = run_of(starts[half], stride)
                rows = slice(half * 8, half * 8 + 8)
                for c in range(x_rows.shape[0]):
                    unit, group = divmod(c, WIDTH // LANES)
                    change = update[unit][rows, lane(group)] + entry(
                        table, self.unit, POINT, lane(c)
                    )
                    current = rounded(x_rows[c, where, :] + change)
                    x_next[c, where, :] = current
                    if s_next is not None:
                        s_next[c, where, :] = snake_in(table, self.unit + 1, c, current)

        for first, length in self.pieces:
            for j in range(length):
                cost = 25 if s_next is None else 50
                steps.append(
                    (cost, functools.partial(step, len(steps), first, j, length))
                )
        return steps


def run_of(start, stride):
    return pl.ds(start, 8) if stride == 1 else pl.ds(start, 8, stride=stride)


def snake_in(table, unit, c, values):
    return snake(values, rates(table, unit, IN, lane(c)))


def weave(main, others=(), own=(), lead=0):
    whole = sum(cost for cost, _ in others)
    spent, at = 0, 0
    for i, (_, step) in enumerate(main):
        step()
        if i // 2 + 1 < len(own):
            late = own[i // 2 + 1]
            run(late[: len(late) // 2] if i % 2 == 0 else late[len(late) // 2 :])
        share = max(0, i + 1 - lead) / (len(main) - lead)
        while at < len(others) and (i + 1 == len(main) or spent < whole * share):
            spent += others[at][0]
            others[at][1]()
            at += 1


def run(steps):
    for _, step in steps:
        step()


def halves(channels):
    return slice(0, channels // 2), slice(channels // 2, channels)


def parts(frames):
    inner = (
        Part(0, [(8, frames // SEGMENTS - 6)]),
        Part(1, [(20, frames // SEGMENTS - 7)]),
        Part(2, [(48, frames // SEGMENTS - 11)]),
    )
    outer = (
        Part(0, [(-36, 3), (frames - 88, 8)]),
        Part(1, [(-28, 3), (frames - 100, 8)], plain=True),
        Part(2, [(0, 3), (frames - 128, 8)], plain=True),
    )
    return inner, outer


def place():
    return lax.axis_index("tm")


def edges_kernel(up_hbm, to_far, to_near, held, sems):
    frames = up_hbm.shape[1]
    copies = []
    for part in range(2):
        for end, row in enumerate((0, frames - SENT)):
            copies.append(
                pltpu.make_async_copy(
                    up_hbm.at[part, pl.ds(row, SENT)], held.at[part, end], sems.at[part, end]
                )
            )
    for copy in copies:
        copy.start()
    for copy in copies:
        copy.wait()
    odd = place() % 2 == 1
    for c in range(up_hbm.shape[2] // LANES):
        own_low, own_high = (held[0, end, :, lane(c)].astype(jnp.float32) for end in range(2))
        low, high = (held[1, end, :, lane(c)].astype(jnp.float32) for end in range(2))
        none = jnp.zeros((STRIDE, LANES), jnp.float32)
        to_next = jnp.concatenate([own_high[STRIDE:], none], axis=0) + high
        to_last = own_low + jnp.concatenate([none, low[:HALO]], axis=0)
        to_far[:, lane(c)] = jnp.where(odd, to_next, to_last).astype(jnp.bfloat16)
        to_near[:, lane(c)] = jnp.where(odd, to_last, to_next).astype(jnp.bfloat16)


def first_kernel(
    up, wide, point, alpha_in, beta_in, alpha_mid, beta_mid, x_rows, s_rows, tiles, table
):
    frames = up.shape[1]
    rows = []
    for alpha, beta in ((alpha_in, beta_in), (alpha_mid, beta_mid)):
        root = jnp.sqrt(1 / beta[...])
        rows += [alpha[...] / math.pi] + [root * coefficient for coefficient in SINE]
    for which, value in enumerate(rows + [wide[...], point[...]]):
        for unit in range(UNITS):
            row = unit * TABLE + which
            table[row : row + 1, :] = value[unit : unit + 1, :]
    for c in range(x_rows.shape[0]):
        later = up[1, :, lane(c)].astype(jnp.float32)
        none = jnp.zeros((STRIDE, LANES), jnp.float32)
        own = up[0, :, lane(c)].astype(jnp.float32)
        current = rounded(own + jnp.concatenate([none, later[: frames - STRIDE]], axis=0))
        table[UNITS * TABLE :, lane(c)] = later[frames - STRIDE :]
        x_rows[c, LEFT : LEFT + frames, :] = current
        s_rows[c, LEFT : LEFT + frames, :] = snake_in(table, 0, c, current)
    run(sum(parts(frames)[0][0].gather(s_rows, tiles), []))


def inner_kernel(frames, tiles, table, taps, middle, gated):
    part = parts(frames)[0][0]
    first, _ = halves(middle.shape[1])
    steps = part.conv(tiles, taps, middle)
    weave(steps[:KERNEL])
    weave(steps[KERNEL:], part.gate(middle, gated, table, first))


def outer_kernel(
    tracks,
    x_first, s_first, first_middle, first_gated, from_chip, from_far, table, taps, point,
    out,
    x_0, x_1, x_2, s_0, s_1, s_2, inner_tiles, outer_tiles, gated,
):
    inner, outer = parts(out.shape[0])

    def sums(*of):
        one = [pltpu.ACC(unit)((SEGMENTS, WIDTH), jnp.float32) for unit in range(2)]
        return [one] * (max(part.rows for part in of) // SEGMENTS)

    def scoped(inner_sums, outer_sums, update_sums):
        outer_body(
            tracks,
            x_first, s_first, first_middle, first_gated, from_chip, from_far, table, taps,
            point, out,
            x_0, x_1, x_2, s_0, s_1, s_2, inner_tiles, outer_tiles, gated,
            inner_sums, outer_sums, update_sums,
        )

    pl.run_scoped(scoped, sums(*inner[1:]), sums(*outer), sums(*inner, *outer))


def outer_body(
    tracks,
    x_first, s_first, first_middle, first_gated, from_chip, from_far, table, taps, point,
    out,
    x_0, x_1, x_2, s_0, s_1, s_2, inner_tiles, outer_tiles, gated,
    inner_sums, outer_sums, update_sums,
):
    frames, channels = out.shape
    groups = x_0.shape[0]
    end_row = LEFT + frames
    odd = place() % 2 == 1
    is_first = place() == 0
    is_last = place() == tracks - 1
    inner, outer = parts(frames)
    both = halves(channels)

    def clear_outside(s_rows):
        def step(c):
            s_rows[c, 0:LEFT, :] = jnp.where(is_first, 0.0, s_rows[c, 0:LEFT, :])
            s_rows[c, end_row:, :] = jnp.where(is_last, 0.0, s_rows[c, end_row:, :])

        return [(10, functools.partial(step, c)) for c in range(groups)]

    def store(begin, end):
        def step(c, row):
            rows = slice(LEFT + row, LEFT + row + SEGMENTS)
            out[row : row + SEGMENTS, lane(c)] = x_0[c, rows, :].astype(jnp.bfloat16)

        return [
            (2, functools.partial(step, c, row))
            for row in range(begin, end, SEGMENTS)
            for c in range(groups)
        ]

    matrix = Matrix()

    def after(part, sums, x_rows, x_next, s_next):
        return (
            part.gate_sums(sums, gated, table)
            + part.project(matrix, [(gated, columns) for columns in both], point, update_sums)
            + part.finish(update_sums, table, x_rows, x_next, s_next)
        )

    low_end = LEFT + 2 * STRIDE
    kept = LEFT + outer[0].pieces[1][0] - 8
    for c in range(groups):
        chip = from_chip[:, lane(c)].astype(jnp.float32)
        far = from_far[:, lane(c)].astype(jnp.float32)
        before = jnp.where(odd, chip, far)
        behind = jnp.where(odd, far, chip)
        carried = jnp.where(is_first, 0.0, before[HALO:SENT])
        own_low = x_first[c, LEFT:low_end, :]
        low = jnp.concatenate(
            [before[:HALO], rounded(own_low[:STRIDE] + carried), own_low[STRIDE:]], axis=0
        )
        joint = rounded(behind[:STRIDE] + table[UNITS * TABLE :, lane(c)])
        high = jnp.concatenate([joint, behind[STRIDE:HALO]], axis=0)
        x_0[c, LEFT - HALO : low_end, :] = low
        s_0[c, LEFT - HALO : low_end, :] = snake_in(table, 0, c, low)
        x_0[c, kept:end_row, :] = x_first[c, kept:end_row, :]
        s_0[c, kept:end_row, :] = s_first[c, kept:end_row, :]
        x_0[c, end_row : end_row + HALO, :] = high
        s_0[c, end_row : end_row + HALO, :] = snake_in(table, 0, c, high)
    run(clear_outside(s_0))
    lead = 1
    own = outer[0].gather(s_0, outer_tiles)
    run(own[0])
    coming = inner[1].gather(s_1, inner_tiles)
    weave(
        outer[0].conv_sums(matrix, outer_tiles, taps, outer_sums),
        inner[0].gate(first_middle, gated, table, both[1])
        + inner[0].project(
            matrix, [(first_gated, both[0]), (gated, both[1])], point, update_sums
        )
        + inner[0].finish(update_sums, table, x_first, x_1, s_1)
        + coming[0],
        own,
    )
    own, coming = coming, outer[1].gather(s_1, outer_tiles)
    weave(
        inner[1].conv_sums(matrix, inner_tiles, taps, inner_sums),
        after(outer[0], outer_sums, x_0, x_1, s_1) + clear_outside(s_1) + coming[0],
        own,
        lead,
    )
    own, coming = coming, inner[2].gather(s_2, inner_tiles)
    weave(
        outer[1].conv_sums(matrix, outer_tiles, taps, outer_sums),
        after(inner[1], inner_sums, x_1, x_2, s_2) + coming[0],
        own,
        lead,
    )
    own, coming = coming, outer[2].gather(s_2, outer_tiles)
    weave(
        inner[2].conv_sums(matrix, inner_tiles, taps, inner_sums),
        after(outer[1], outer_sums, x_1, x_2, s_2) + clear_outside(s_2) + coming[0],
        own,
        lead,
    )
    begin = inner[2].pieces[0][0]
    end = begin + inner[2].rows
    weave(
        outer[2].conv_sums(matrix, outer_tiles, taps, outer_sums),
        after(inner[2], inner_sums, x_2, x_0, None) + store(begin, end),
        coming,
        lead,
    )
    run(after(outer[2], outer_sums, x_2, x_0, None))
    run(store(0, begin) + store(end, frames))


def swaps(groups, count):
    near, far = [], []
    for group in range(groups):
        for index in range(count):
            me = group * count + index
            near.append((me, group * count + (index ^ 1)))
            if index == 0 or index == count - 1:
                far.append((me, (group ^ 1) * count + index))
            else:
                far.append((me, me + 1 if index % 2 else me - 1))
    return near, far


VMEM = pl.BlockSpec(memory_space=pltpu.VMEM)
HBM = pl.BlockSpec(memory_space=pltpu.HBM)


def in_hbm(value):
    return pltpu.with_memory_space_constraint(value, pltpu.HBM)


VMEM = pl.BlockSpec(memory_space=pltpu.VMEM)
HBM = pl.BlockSpec(memory_space=pltpu.HBM)


def in_hbm(value):
    return pltpu.with_memory_space_constraint(value, pltpu.HBM)


def per_device(
    upsampled, taps, bias_wide, pointwise, bias_point, alpha_in, beta_in, alpha_mid, beta_mid
):
    frames, channels = upsampled.shape[1:]
    count = lax.axis_size("tm")
    near, far = swaps(lax.axis_size("grp"), count)
    groups = channels // LANES
    rows = frames + 2 * LEFT
    half = jnp.bfloat16
    params = (bias_wide, bias_point, alpha_in, beta_in, alpha_mid, beta_mid)
    limit = pltpu.CompilerParams(vmem_limit_bytes=16 * 2**20)

    sent = jax.ShapeDtypeStruct((SENT, channels), half)
    to_far, to_near = pl.pallas_call(
        edges_kernel,
        out_shape=(sent, sent),
        in_specs=[HBM],
        out_specs=(VMEM,) * 2,
        scratch_shapes=[
            pltpu.VMEM((2, 2, SENT, channels), half),
            pltpu.SemaphoreType.DMA((2, 2)),
        ],
        compiler_params=limit,
        cost_estimate=pl.CostEstimate(
            flops=6 * 10**9, bytes_accessed=upsampled.size * 2, transcendentals=0
        ),
        name="edges",
    )(in_hbm(upsampled))

    from_far = lax.ppermute(to_far, ("grp", "tm"), far)
    from_chip = lax.ppermute(to_near, ("grp", "tm"), near)

    inner, outer = parts(frames)
    natural = (groups, rows, LANES)
    single = jnp.float32

    def tiles(*of):
        return max(part.tiles for part in of) * SEGMENTS, channels

    def most(*of):
        return max(part.rows for part in of), channels

    x_first, s_first, first_tiles, table = pl.pallas_call(
        first_kernel,
        out_shape=(
            jax.ShapeDtypeStruct(natural, single),
            jax.ShapeDtypeStruct(natural, single),
            jax.ShapeDtypeStruct(tiles(inner[0]), half),
            jax.ShapeDtypeStruct((UNITS * TABLE + STRIDE, channels), single),
        ),
        in_specs=[VMEM] * 7,
        out_specs=(VMEM,) * 4,
        compiler_params=limit,
        name="first",
    )(upsampled, *params)

    first_middle, first_gated = pl.pallas_call(
        functools.partial(inner_kernel, frames),
        out_shape=(
            jax.ShapeDtypeStruct(most(inner[0]), single),
            jax.ShapeDtypeStruct(most(inner[0]), half),
        ),
        in_specs=[VMEM] * 3,
        out_specs=(VMEM,) * 2,
        compiler_params=limit,
        cost_estimate=pl.CostEstimate(
            flops=2 * KERNEL * inner[0].rows * channels**2,
            bytes_accessed=taps.size * 2,
            transcendentals=0,
        ),
        name="inner",
    )(first_tiles, table, taps)

    return pl.pallas_call(
        functools.partial(outer_kernel, count),
        out_shape=jax.ShapeDtypeStruct((frames, channels), half),
        in_specs=[VMEM] * 9,
        out_specs=VMEM,
        scratch_shapes=[pltpu.VMEM(natural, single)] * 6
        + [
            pltpu.VMEM(tiles(*inner[1:]), half),
            pltpu.VMEM(tiles(*outer), half),
            pltpu.VMEM(most(*inner, *outer), half),
        ],
        compiler_params=pltpu.CompilerParams(vmem_limit_bytes=24 * 2**20),
        name="outer",
    )(
        x_first, s_first, first_middle, first_gated, from_chip, from_far,
        table, taps, pointwise,
    )


def solution(mesh):
    placed = (P(None, ("grp", "tm"), None), P(), P(), P(), P(), P(), P(), P(), P())
    return jax.shard_map(
        per_device, mesh=mesh, in_specs=placed, out_specs=P(("grp", "tm"), None), check_vma=False
    )
```

```python
import functools
import math

import jax
import jax.numpy as jnp
from jax import lax
from jax.experimental import pallas as pl
from jax.experimental.pallas import tpu as pltpu
from jax.sharding import PartitionSpec as P

KERNEL = 7
STRIDE = 8
UNITS = 3
DILATIONS = (1, 3, 9)
LANES = 128
LEFT = 48
SENT = 48
HALO = 40
SEGMENTS = 16
TABLE = 16
IN, MID, WIDE, POINT = 0, 5, 10, 11

SINE = (3.141582022, -5.167142795, 2.541899018, -0.5546361724)


def snake(values, rates):
    turns = values * rates[0]
    rest = turns - jnp.round(turns)
    square = rest * rest
    sine = rates[-1]
    for coefficient in rates[-2:0:-1]:
        sine = sine * square + coefficient
    sine = sine * rest
    return values + sine * sine


def rounded(values):
    return values.astype(jnp.bfloat16).astype(jnp.float32)


def lane(c):
    return slice(c * LANES, (c + 1) * LANES)


def entry(table, unit, which, lanes=slice(None)):
    row = unit * TABLE + which
    return table[row : row + 1, lanes]


WIDTH = 256


def rates(table, unit, which, lanes):
    return [entry(table, unit, which + i, lanes) for i in range(5)]


class Matrix:
    def __init__(self):
        self.count = 0
        self.staged = None

    def tile(self, weights, rows, sums):
        register = self.count % 2
        self.count += 1
        for unit in range(2):
            pltpu.matmul_push_rhs(weights(unit), register, unit)
        self.flush()
        self.staged = register, rows, sums

    def flush(self):
        if self.staged is None:
            return
        register, rows, sums = self.staged
        self.staged = None
        for i, pair in enumerate(sums):
            for unit in range(2):
                load = register if i == 0 else None
                pltpu.matmul_acc_lhs(pair[unit], rows(unit, i), load_staged_rhs=load)


class Part:
    def __init__(self, unit, pieces, plain=False):
        self.unit = unit
        self.plain = plain
        self.dilation = DILATIONS[unit]
        self.pieces = pieces
        self.rows = SEGMENTS * sum(length for _, length in pieces)
        if plain:
            self.tiles = KERNEL * self.rows // SEGMENTS
        else:
            self.tiles = sum(length + 6 * self.dilation for _, length in pieces)

    def starts(self, first, j, length):
        if self.plain:
            start = LEFT + first + SEGMENTS * j
            return (start, start + 8), 1
        start = LEFT + first + j
        return (start, start + 8 * length), length

    def gather(self, s_rows, tiles):
        steps = [[] for _ in range(KERNEL)]

        def step(at, first, j, length):
            rows = slice(at * SEGMENTS, (at + 1) * SEGMENTS)
            starts, stride = self.starts(first, j, length)
            for c in range(s_rows.shape[0]):
                both = [s_rows[c, run_of(start, stride), :] for start in starts]
                tiles[rows, lane(c)] = jnp.concatenate(both, axis=0).astype(jnp.bfloat16)

        reach = 3 * self.dilation
        for k in range(KERNEL):
            at = 0
            for first, length in self.pieces:
                if self.plain:
                    away = first + (k - 3) * self.dilation
                    new = [(k * self.rows // SEGMENTS + at + j, away, j) for j in range(length)]
                    at += length
                else:
                    begin = length + (k - 1) * self.dilation if k else 0
                    end = length + k * self.dilation
                    new = [(at + j, first - reach, j) for j in range(begin, end)]
                    at += length + 2 * reach
                for tile, start, j in new:
                    steps[k].append((10, functools.partial(step, tile, start, j, length)))
        return steps

    def window(self, tiles, k):
        at, found = 0, []
        for _, length in self.pieces:
            row = (at + k * self.dilation) * SEGMENTS
            found.append(tiles[row : row + length * SEGMENTS, :])
            at += length + 6 * self.dilation
        return found[0] if len(found) == 1 else jnp.concatenate(found, axis=0)

    def conv(self, tiles, taps, middle):
        channels = middle.shape[1]
        total = [None]

        def step(columns, k):
            product = jnp.dot(
                self.window(tiles, k),
                taps[self.unit, k, :, columns],
                preferred_element_type=jnp.float32,
            )
            total[0] = product if k == 0 else total[0] + product
            if k == KERNEL - 1:
                middle[: self.rows, columns] = total[0]

        return [
            (1, functools.partial(step, columns, k))
            for columns in halves(channels)
            for k in range(KERNEL)
        ]

    def conv_sums(self, matrix, tiles, taps, sums, columns=None):
        places, at = [], 0
        for _, length in self.pieces:
            places += range(at, at + length)
            at += length + (0 if self.plain else 6 * self.dilation)
        away = len(places) if self.plain else self.dilation

        both = halves(taps.shape[2])

        def rows(k, inputs, i):
            row = (places[i] + k * away) * SEGMENTS
            return tiles[row : row + SEGMENTS, inputs]

        def step(k, inputs):
            matrix.tile(
                lambda unit: taps[self.unit, k, inputs, both[unit]],
                lambda unit, i: rows(k, inputs, i),
                sums[: len(places)],
            )

        def column_step(k):
            matrix.tile(
                lambda unit: taps[self.unit, k, both[unit], columns],
                lambda unit, i: rows(k, both[unit], i),
                sums[: len(places)],
            )

        if columns is not None:
            return [(1, functools.partial(column_step, k)) for k in range(KERNEL)]
        steps = [
            (1, functools.partial(step, k, inputs)) for k in range(KERNEL) for inputs in both
        ]
        return steps + [(1, matrix.flush)]

    def gate_values(self, values, gated, table, columns):
        gated_values = snake(
            values + entry(table, self.unit, WIDE, columns),
            rates(table, self.unit, MID, columns),
        )
        return gated_values.astype(jnp.bfloat16)

    def gate(self, middle, gated, table, columns):
        def step(rows):
            gated[rows, columns] = self.gate_values(middle[rows, columns], gated, table, columns)

        return [
            (20, functools.partial(step, slice(row, row + SEGMENTS)))
            for row in range(0, self.rows, SEGMENTS)
        ]

    def gate_sums(self, sums, gated, table):
        def step(i):
            rows = slice(i * SEGMENTS, (i + 1) * SEGMENTS)
            for unit, columns in enumerate(halves(gated.shape[1])):
                values = pltpu.matmul_pop(sums[i][unit])
                gated[rows, columns] = self.gate_values(values, gated, table, columns)

        return [(20, functools.partial(step, i)) for i in range(self.rows // SEGMENTS)]

    def gate_columns(self, sums, gated, table, columns):
        def step(i):
            rows = slice(i * SEGMENTS, (i + 1) * SEGMENTS)
            values = pltpu.matmul_pop(sums[i][0]) + pltpu.matmul_pop(sums[i][1])
            gated[rows, columns] = self.gate_values(values, gated, table, columns)

        return [(20, functools.partial(step, i)) for i in range(self.rows // SEGMENTS)]

    def project(self, matrix, sources, point, sums):
        def rows(gated, columns, i):
            return gated[i * SEGMENTS : (i + 1) * SEGMENTS, columns]

        both = halves(point.shape[2])

        def step(gated, inputs):
            matrix.tile(
                lambda unit: point[self.unit, inputs, both[unit]],
                lambda unit, i: rows(gated, inputs, i),
                sums[: self.rows // SEGMENTS],
            )

        steps = [(5, functools.partial(step, gated, columns)) for gated, columns in sources]
        return steps + [(5, matrix.flush)]

    def finish(self, sums, table, x_rows, x_next, s_next=None):
        steps = []

        def step(i, first, j, length):
            starts, stride = self.starts(first, j, length)
            update = [pltpu.matmul_pop(sums[i][unit]) for unit in range(2)]
            for half in range(2):
                where = run_of(starts[half], stride)
                rows = slice(half * 8, half * 8 + 8)
                for c in range(x_rows.shape[0]):
                    unit, group = divmod(c, WIDTH // LANES)
                    change = update[unit][rows, lane(group)] + entry(
                        table, self.unit, POINT, lane(c)
                    )
                    current = rounded(x_rows[c, where, :] + change)
                    x_next[c, where, :] = current
                    if s_next is not None:
                        s_next[c, where, :] = snake_in(table, self.unit + 1, c, current)

        for first, length in self.pieces:
            for j in range(length):
                cost = 25 if s_next is None else 50
                steps.append(
                    (cost, functools.partial(step, len(steps), first, j, length))
                )
        return steps


def run_of(start, stride):
    return pl.ds(start, 8) if stride == 1 else pl.ds(start, 8, stride=stride)


def snake_in(table, unit, c, values):
    return snake(values, rates(table, unit, IN, lane(c)))


def weave(main, others=(), own=(), lead=0):
    pace = 1 if len(main) == KERNEL else 2
    whole = sum(cost for cost, _ in others)
    spent, at = 0, 0
    for i, (_, step) in enumerate(main):
        step()
        if i // pace + 1 < len(own):
            late = own[i // pace + 1]
            run(late[i % pace :: pace])
        share = max(0, i + 1 - lead) / (len(main) - lead)
        while at < len(others) and (i + 1 == len(main) or spent < whole * share):
            spent += others[at][0]
            others[at][1]()
            at += 1


def run(steps):
    for _, step in steps:
        step()


def halves(channels):
    return slice(0, channels // 2), slice(channels // 2, channels)


def parts(frames):
    inner = (
        Part(0, [(8, frames // SEGMENTS - 6)]),
        Part(1, [(20, frames // SEGMENTS - 7)]),
        Part(2, [(48, frames // SEGMENTS - 11)]),
    )
    outer = (
        Part(0, [(-36, 3), (frames - 88, 8)]),
        Part(1, [(-28, 3), (frames - 100, 8)], plain=True),
        Part(2, [(0, 3), (frames - 128, 8)], plain=True),
    )
    return inner, outer


def place():
    return lax.axis_index("tm")


def edges_kernel(up_hbm, to_far, to_near, held, sems):
    frames = up_hbm.shape[1]
    copies = []
    for part in range(2):
        for end, row in enumerate((0, frames - SENT)):
            copies.append(
                pltpu.make_async_copy(
                    up_hbm.at[part, pl.ds(row, SENT)], held.at[part, end], sems.at[part, end]
                )
            )
    for copy in copies:
        copy.start()
    for copy in copies:
        copy.wait()
    odd = place() % 2 == 1
    for c in range(up_hbm.shape[2] // LANES):
        own_low, own_high = (held[0, end, :, lane(c)].astype(jnp.float32) for end in range(2))
        low, high = (held[1, end, :, lane(c)].astype(jnp.float32) for end in range(2))
        none = jnp.zeros((STRIDE, LANES), jnp.float32)
        to_next = jnp.concatenate([own_high[STRIDE:], none], axis=0) + high
        to_last = own_low + jnp.concatenate([none, low[:HALO]], axis=0)
        to_far[:, lane(c)] = jnp.where(odd, to_next, to_last).astype(jnp.bfloat16)
        to_near[:, lane(c)] = jnp.where(odd, to_last, to_next).astype(jnp.bfloat16)


def first_kernel(
    up, wide, point, alpha_in, beta_in, alpha_mid, beta_mid, x_rows, s_rows, tiles, table
):
    frames = up.shape[1]
    rows = []
    for alpha, beta in ((alpha_in, beta_in), (alpha_mid, beta_mid)):
        root = jnp.sqrt(1 / beta[...])
        rows += [alpha[...] / math.pi] + [root * coefficient for coefficient in SINE]
    for which, value in enumerate(rows + [wide[...], point[...]]):
        for unit in range(UNITS):
            row = unit * TABLE + which
            table[row : row + 1, :] = value[unit : unit + 1, :]
    for c in range(x_rows.shape[0]):
        later = up[1, :, lane(c)].astype(jnp.float32)
        none = jnp.zeros((STRIDE, LANES), jnp.float32)
        own = up[0, :, lane(c)].astype(jnp.float32)
        current = rounded(own + jnp.concatenate([none, later[: frames - STRIDE]], axis=0))
        table[UNITS * TABLE :, lane(c)] = later[frames - STRIDE :]
        x_rows[c, LEFT : LEFT + frames, :] = current
        s_rows[c, LEFT : LEFT + frames, :] = snake_in(table, 0, c, current)
    run(sum(parts(frames)[0][0].gather(s_rows, tiles), []))


def inner_kernel(frames, tiles, table, taps, middle, gated):
    part = parts(frames)[0][0]
    first, _ = halves(middle.shape[1])
    steps = part.conv(tiles, taps, middle)
    weave(steps[:KERNEL])
    weave(steps[KERNEL:], part.gate(middle, gated, table, first))


def outer_kernel(
    tracks,
    x_first, s_first, first_middle, first_gated, from_chip, from_far, table, taps, point,
    out,
    x_0, x_1, x_2, s_0, s_1, s_2, inner_tiles, outer_tiles, gated, gated_2, held, sems,
):
    inner, outer = parts(out.shape[0])

    def sums(*of):
        one = [pltpu.ACC(unit)((SEGMENTS, WIDTH), jnp.float32) for unit in range(2)]
        return [one] * (max(part.rows for part in of) // SEGMENTS)

    def scoped(inner_sums, outer_sums, last_sums, update_sums):
        outer_body(
            tracks,
            x_first, s_first, first_middle, first_gated, from_chip, from_far, table, taps,
            point, out,
            x_0, x_1, x_2, s_0, s_1, s_2, inner_tiles, outer_tiles, gated, gated_2, held, sems,
            inner_sums, outer_sums, last_sums, update_sums,
        )

    pl.run_scoped(
        scoped, sums(*inner[1:]), sums(*outer), sums(outer[2]), sums(*inner, *outer)
    )


def outer_body(
    tracks,
    x_first, s_first, first_middle, first_gated, from_chip, from_far, table, taps, point,
    out,
    x_0, x_1, x_2, s_0, s_1, s_2, inner_tiles, outer_tiles, gated, gated_2, held, sems,
    inner_sums, outer_sums, last_sums, update_sums,
):
    frames, channels = out.shape
    groups = x_0.shape[0]
    end_row = LEFT + frames
    odd = place() % 2 == 1
    is_first = place() == 0
    is_last = place() == tracks - 1
    inner, outer = parts(frames)
    both = halves(channels)

    def clear_outside(s_rows):
        def step(c):
            s_rows[c, 0:LEFT, :] = jnp.where(is_first, 0.0, s_rows[c, 0:LEFT, :])
            s_rows[c, end_row:, :] = jnp.where(is_last, 0.0, s_rows[c, end_row:, :])

        return [(10, functools.partial(step, c)) for c in range(groups)]

    copies = []

    def send(begin, end):
        def step():
            rows = pl.ds(begin, end - begin)
            copy = pltpu.make_async_copy(held.at[rows], out.at[rows], sems.at[len(copies)])
            copies.append(copy)
            copy.start()

        return step

    def store(begin, end):
        def step(c, row):
            rows = slice(LEFT + row, LEFT + row + SEGMENTS)
            held[row : row + SEGMENTS, lane(c)] = x_0[c, rows, :].astype(jnp.bfloat16)

        return [
            (2, functools.partial(step, c, row))
            for row in range(begin, end, SEGMENTS)
            for c in range(groups)
        ]

    matrix = Matrix()

    def after(part, sums, x_rows, x_next, s_next):
        return (
            part.gate_sums(sums, gated, table)
            + part.project(matrix, [(gated, columns) for columns in both], point, update_sums)
            + part.finish(update_sums, table, x_rows, x_next, s_next)
        )

    low_end = LEFT + 2 * STRIDE
    kept = LEFT + outer[0].pieces[1][0] - 8
    for c in range(groups):
        chip = from_chip[:, lane(c)].astype(jnp.float32)
        far = from_far[:, lane(c)].astype(jnp.float32)
        before = jnp.where(odd, chip, far)
        behind = jnp.where(odd, far, chip)
        carried = jnp.where(is_first, 0.0, before[HALO:SENT])
        own_low = x_first[c, LEFT:low_end, :]
        low = jnp.concatenate(
            [before[:HALO], rounded(own_low[:STRIDE] + carried), own_low[STRIDE:]], axis=0
        )
        joint = rounded(behind[:STRIDE] + table[UNITS * TABLE :, lane(c)])
        high = jnp.concatenate([joint, behind[STRIDE:HALO]], axis=0)
        x_0[c, LEFT - HALO : low_end, :] = low
        s_0[c, LEFT - HALO : low_end, :] = snake_in(table, 0, c, low)
        x_0[c, kept:end_row, :] = x_first[c, kept:end_row, :]
        s_0[c, kept:end_row, :] = s_first[c, kept:end_row, :]
        x_0[c, end_row : end_row + HALO, :] = high
        s_0[c, end_row : end_row + HALO, :] = snake_in(table, 0, c, high)
    run(clear_outside(s_0))
    lead = 1
    own = outer[0].gather(s_0, outer_tiles)
    run(own[0])
    coming = inner[1].gather(s_1, inner_tiles)
    weave(
        outer[0].conv_sums(matrix, outer_tiles, taps, outer_sums),
        inner[0].gate(first_middle, gated, table, both[1])
        + inner[0].project(
            matrix, [(first_gated, both[0]), (gated, both[1])], point, update_sums
        )
        + inner[0].finish(update_sums, table, x_first, x_1, s_1)
        + coming[0],
        own,
    )
    own, coming = coming, outer[1].gather(s_1, outer_tiles)
    weave(
        inner[1].conv_sums(matrix, inner_tiles, taps, inner_sums),
        after(outer[0], outer_sums, x_0, x_1, s_1) + clear_outside(s_1) + coming[0],
        own,
        lead,
    )
    own, coming = coming, inner[2].gather(s_2, inner_tiles)
    weave(
        outer[1].conv_sums(matrix, outer_tiles, taps, outer_sums),
        after(inner[1], inner_sums, x_1, x_2, s_2) + coming[0],
        own,
        lead,
    )
    own, coming = coming, outer[2].gather(s_2, outer_tiles)
    weave(
        inner[2].conv_sums(matrix, inner_tiles, taps, inner_sums),
        after(outer[1], outer_sums, x_1, x_2, s_2) + clear_outside(s_2) + coming[0],
        own,
        lead,
    )
    begin = inner[2].pieces[0][0]
    end = begin + inner[2].rows
    last = outer[2]
    finish = after(inner[2], inner_sums, x_2, x_0, None) + store(begin, end)
    finish.append((2, send(begin, end)))
    cut = len(finish) // 2
    sums = outer_sums, last_sums
    conv = [
        last.conv_sums(matrix, outer_tiles, taps, sums[n], columns)
        for n, columns in enumerate(both)
    ]
    point_steps = last.project(matrix, [(gated_2, columns) for columns in both], point, update_sums)
    weave(conv[0], finish[:cut], coming, lead)
    weave(conv[1], finish[cut:] + last.gate_columns(sums[0], gated_2, table, both[0]))
    run(point_steps[:1])
    run(last.gate_columns(sums[1], gated_2, table, both[1]))
    run(point_steps[1:])
    run(last.finish(update_sums, table, x_2, x_0))
    run(store(0, begin) + [(2, send(0, begin))] + store(end, frames) + [(2, send(end, frames))])
    for copy in copies:
        copy.wait()


def swaps(groups, count):
    near, far = [], []
    for group in range(groups):
        for index in range(count):
            me = group * count + index
            near.append((me, group * count + (index ^ 1)))
            if index == 0 or index == count - 1:
                far.append((me, (group ^ 1) * count + index))
            else:
                far.append((me, me + 1 if index % 2 else me - 1))
    return near, far


VMEM = pl.BlockSpec(memory_space=pltpu.VMEM)
HBM = pl.BlockSpec(memory_space=pltpu.HBM)


def in_hbm(value):
    return pltpu.with_memory_space_constraint(value, pltpu.HBM)


VMEM = pl.BlockSpec(memory_space=pltpu.VMEM)
HBM = pl.BlockSpec(memory_space=pltpu.HBM)


def in_hbm(value):
    return pltpu.with_memory_space_constraint(value, pltpu.HBM)


def per_device(
    upsampled, taps, bias_wide, pointwise, bias_point, alpha_in, beta_in, alpha_mid, beta_mid
):
    frames, channels = upsampled.shape[1:]
    count = lax.axis_size("tm")
    near, far = swaps(lax.axis_size("grp"), count)
    groups = channels // LANES
    rows = frames + 2 * LEFT
    half = jnp.bfloat16
    params = (bias_wide, bias_point, alpha_in, beta_in, alpha_mid, beta_mid)
    limit = pltpu.CompilerParams(vmem_limit_bytes=16 * 2**20)

    sent = jax.ShapeDtypeStruct((SENT, channels), half)
    to_far, to_near = pl.pallas_call(
        edges_kernel,
        out_shape=(sent, sent),
        in_specs=[HBM],
        out_specs=(VMEM,) * 2,
        scratch_shapes=[
            pltpu.VMEM((2, 2, SENT, channels), half),
            pltpu.SemaphoreType.DMA((2, 2)),
        ],
        compiler_params=limit,
        cost_estimate=pl.CostEstimate(
            flops=6 * 10**9, bytes_accessed=upsampled.size * 2, transcendentals=0
        ),
        name="edges",
    )(in_hbm(upsampled))

    from_far = lax.ppermute(to_far, ("grp", "tm"), far)
    from_chip = lax.ppermute(to_near, ("grp", "tm"), near)

    inner, outer = parts(frames)
    natural = (groups, rows, LANES)
    single = jnp.float32

    def tiles(*of):
        return max(part.tiles for part in of) * SEGMENTS, channels

    def most(*of):
        return max(part.rows for part in of), channels

    x_first, s_first, first_tiles, table = pl.pallas_call(
        first_kernel,
        out_shape=(
            jax.ShapeDtypeStruct(natural, single),
            jax.ShapeDtypeStruct(natural, single),
            jax.ShapeDtypeStruct(tiles(inner[0]), half),
            jax.ShapeDtypeStruct((UNITS * TABLE + STRIDE, channels), single),
        ),
        in_specs=[VMEM] * 7,
        out_specs=(VMEM,) * 4,
        compiler_params=limit,
        name="first",
    )(upsampled, *params)

    first_middle, first_gated = pl.pallas_call(
        functools.partial(inner_kernel, frames),
        out_shape=(
            jax.ShapeDtypeStruct(most(inner[0]), single),
            jax.ShapeDtypeStruct(most(inner[0]), half),
        ),
        in_specs=[VMEM] * 3,
        out_specs=(VMEM,) * 2,
        compiler_params=limit,
        cost_estimate=pl.CostEstimate(
            flops=2 * KERNEL * inner[0].rows * channels**2,
            bytes_accessed=taps.size * 2,
            transcendentals=0,
        ),
        name="inner",
    )(first_tiles, table, taps)

    return pl.pallas_call(
        functools.partial(outer_kernel, count),
        out_shape=jax.ShapeDtypeStruct((frames, channels), half),
        in_specs=[VMEM] * 9,
        out_specs=HBM,
        scratch_shapes=[pltpu.VMEM(natural, single)] * 6
        + [
            pltpu.VMEM(tiles(*inner[1:]), half),
            pltpu.VMEM(tiles(*outer), half),
            pltpu.VMEM(most(*inner, *outer), half),
            pltpu.VMEM(most(outer[2]), half),
            pltpu.VMEM((frames, channels), half),
            pltpu.SemaphoreType.DMA((3,)),
        ],
        compiler_params=pltpu.CompilerParams(vmem_limit_bytes=24 * 2**20),
        name="outer",
    )(
        x_first, s_first, first_middle, first_gated, from_chip, from_far,
        table, taps, pointwise,
    )


def solution(mesh):
    placed = (P(None, ("grp", "tm"), None), P(), P(), P(), P(), P(), P(), P(), P())
    return jax.shard_map(
        per_device, mesh=mesh, in_specs=placed, out_specs=P(("grp", "tm"), None), check_vma=False
    )
```

```python
import functools
import math

import jax
import jax.numpy as jnp
from jax import lax
from jax.experimental import pallas as pl
from jax.experimental.pallas import tpu as pltpu
from jax.sharding import PartitionSpec as P

KERNEL = 7
STRIDE = 8
UNITS = 3
DILATIONS = (1, 3, 9)
LANES = 128
LEFT = 48
SENT = 48
HALO = 40
LATE = 64
SEGMENTS = 16
TABLE = 16
IN, MID, WIDE, POINT = 0, 5, 10, 11

SINE = (3.141582022, -5.167142795, 2.541899018, -0.5546361724)


def snake(values, rates):
    turns = values * rates[0]
    rest = turns - jnp.round(turns)
    square = rest * rest
    sine = rates[-1]
    for coefficient in rates[-2:0:-1]:
        sine = sine * square + coefficient
    sine = sine * rest
    return values + sine * sine


def rounded(values):
    return values.astype(jnp.bfloat16).astype(jnp.float32)


def lane(c):
    return slice(c * LANES, (c + 1) * LANES)


def entry(table, unit, which, lanes=slice(None)):
    row = unit * TABLE + which
    return table[row : row + 1, lanes]


WIDTH = 256


def rates(table, unit, which, lanes):
    return [entry(table, unit, which + i, lanes) for i in range(5)]


class Matrix:
    def __init__(self):
        self.count = 0
        self.staged = None

    def tile(self, weights, rows, sums):
        register = self.count % 2
        self.count += 1
        for unit in range(2):
            pltpu.matmul_push_rhs(weights(unit), register, unit)
        self.flush()
        self.staged = register, rows, sums

    def flush(self):
        if self.staged is None:
            return
        register, rows, sums = self.staged
        self.staged = None
        for i, pair in enumerate(sums):
            for unit in range(2):
                load = register if i == 0 else None
                pltpu.matmul_acc_lhs(pair[unit], rows(unit, i), load_staged_rhs=load)


class Part:
    def __init__(self, unit, pieces, plain=False):
        self.unit = unit
        self.plain = plain
        self.dilation = DILATIONS[unit]
        self.pieces = pieces
        self.rows = SEGMENTS * sum(length for _, length in pieces)
        if plain:
            self.tiles = KERNEL * self.rows // SEGMENTS
        else:
            self.tiles = sum(length + 6 * self.dilation for _, length in pieces)

    def starts(self, first, j, length):
        if self.plain:
            start = LEFT + first + SEGMENTS * j
            return (start, start + 8), 1
        start = LEFT + first + j
        return (start, start + 8 * length), length

    def gather(self, s_rows, tiles):
        steps = [[] for _ in range(KERNEL)]

        def step(at, first, j, length):
            rows = slice(at * SEGMENTS, (at + 1) * SEGMENTS)
            starts, stride = self.starts(first, j, length)
            for c in range(s_rows.shape[0]):
                both = [s_rows[c, run_of(start, stride), :] for start in starts]
                tiles[rows, lane(c)] = jnp.concatenate(both, axis=0).astype(jnp.bfloat16)

        reach = 3 * self.dilation
        for k in range(KERNEL):
            at = 0
            for first, length in self.pieces:
                if self.plain:
                    away = first + (k - 3) * self.dilation
                    new = [(k * self.rows // SEGMENTS + at + j, away, j) for j in range(length)]
                    at += length
                else:
                    begin = length + (k - 1) * self.dilation if k else 0
                    end = length + k * self.dilation
                    new = [(at + j, first - reach, j) for j in range(begin, end)]
                    at += length + 2 * reach
                for tile, start, j in new:
                    steps[k].append((10, functools.partial(step, tile, start, j, length)))
        return steps

    def window(self, tiles, k):
        at, found = 0, []
        for _, length in self.pieces:
            row = (at + k * self.dilation) * SEGMENTS
            found.append(tiles[row : row + length * SEGMENTS, :])
            at += length + 6 * self.dilation
        return found[0] if len(found) == 1 else jnp.concatenate(found, axis=0)

    def conv(self, tiles, taps, middle):
        channels = middle.shape[1]
        total = [None]

        def step(columns, k):
            product = jnp.dot(
                self.window(tiles, k),
                taps[self.unit, k, :, columns],
                preferred_element_type=jnp.float32,
            )
            total[0] = product if k == 0 else total[0] + product
            if k == KERNEL - 1:
                middle[: self.rows, columns] = total[0]

        return [
            (1, functools.partial(step, columns, k))
            for columns in halves(channels)
            for k in range(KERNEL)
        ]

    def conv_sums(self, matrix, tiles, taps, sums, columns=None):
        places, at = [], 0
        for _, length in self.pieces:
            places += range(at, at + length)
            at += length + (0 if self.plain else 6 * self.dilation)
        away = len(places) if self.plain else self.dilation

        both = halves(taps.shape[2])

        def rows(k, inputs, i):
            row = (places[i] + k * away) * SEGMENTS
            return tiles[row : row + SEGMENTS, inputs]

        def step(k, inputs):
            matrix.tile(
                lambda unit: taps[self.unit, k, inputs, both[unit]],
                lambda unit, i: rows(k, inputs, i),
                sums[: len(places)],
            )

        def column_step(k):
            matrix.tile(
                lambda unit: taps[self.unit, k, both[unit], columns],
                lambda unit, i: rows(k, both[unit], i),
                sums[: len(places)],
            )

        if columns is not None:
            return [(1, functools.partial(column_step, k)) for k in range(KERNEL)]
        steps = [
            (1, functools.partial(step, k, inputs)) for k in range(KERNEL) for inputs in both
        ]
        return steps + [(1, matrix.flush)]

    def gate_values(self, values, gated, table, columns):
        gated_values = snake(
            values + entry(table, self.unit, WIDE, columns),
            rates(table, self.unit, MID, columns),
        )
        return gated_values.astype(jnp.bfloat16)

    def gate(self, middle, gated, table, columns):
        def step(rows):
            gated[rows, columns] = self.gate_values(middle[rows, columns], gated, table, columns)

        return [
            (20, functools.partial(step, slice(row, row + SEGMENTS)))
            for row in range(0, self.rows, SEGMENTS)
        ]

    def gate_sums(self, sums, gated, table):
        def step(i):
            rows = slice(i * SEGMENTS, (i + 1) * SEGMENTS)
            for unit, columns in enumerate(halves(gated.shape[1])):
                values = pltpu.matmul_pop(sums[i][unit])
                gated[rows, columns] = self.gate_values(values, gated, table, columns)

        return [(20, functools.partial(step, i)) for i in range(self.rows // SEGMENTS)]

    def finish_plain(self, sums, table, x_rows, out):
        steps = []

        def step(i, first, j):
            row = first + SEGMENTS * j
            for c in range(x_rows.shape[0]):
                unit, group = divmod(c, WIDTH // LANES)
                if group == 0:
                    update = pltpu.matmul_pop(sums[i][unit])
                change = update[:, lane(group)] + entry(table, self.unit, POINT, lane(c))
                current = x_rows[c, LEFT + row : LEFT + row + SEGMENTS, :] + change
                out[row : row + SEGMENTS, lane(c)] = current.astype(jnp.bfloat16)

        for first, length in self.pieces:
            for j in range(length):
                steps.append((20, functools.partial(step, len(steps), first, j)))
        return steps

    def gate_columns(self, sums, gated, table, columns):
        def step(i):
            rows = slice(i * SEGMENTS, (i + 1) * SEGMENTS)
            values = pltpu.matmul_pop(sums[i][0]) + pltpu.matmul_pop(sums[i][1])
            gated[rows, columns] = self.gate_values(values, gated, table, columns)

        return [(20, functools.partial(step, i)) for i in range(self.rows // SEGMENTS)]

    def project(self, matrix, sources, point, sums):
        def rows(gated, columns, i):
            return gated[i * SEGMENTS : (i + 1) * SEGMENTS, columns]

        both = halves(point.shape[2])

        def step(gated, inputs):
            matrix.tile(
                lambda unit: point[self.unit, inputs, both[unit]],
                lambda unit, i: rows(gated, inputs, i),
                sums[: self.rows // SEGMENTS],
            )

        steps = [(5, functools.partial(step, gated, columns)) for gated, columns in sources]
        return steps + [(5, matrix.flush)]

    def finish(self, sums, table, x_rows, x_next, s_next=None):
        steps = []

        def step(i, first, j, length):
            starts, stride = self.starts(first, j, length)
            update = [pltpu.matmul_pop(sums[i][unit]) for unit in range(2)]
            for half in range(2):
                where = run_of(starts[half], stride)
                rows = slice(half * 8, half * 8 + 8)
                for c in range(x_rows.shape[0]):
                    unit, group = divmod(c, WIDTH // LANES)
                    change = update[unit][rows, lane(group)] + entry(
                        table, self.unit, POINT, lane(c)
                    )
                    current = rounded(x_rows[c, where, :] + change)
                    x_next[c, where, :] = current
                    if s_next is not None:
                        s_next[c, where, :] = snake_in(table, self.unit + 1, c, current)

        for first, length in self.pieces:
            for j in range(length):
                cost = 25 if s_next is None else 50
                steps.append(
                    (cost, functools.partial(step, len(steps), first, j, length))
                )
        return steps


def run_of(start, stride):
    return pl.ds(start, 8) if stride == 1 else pl.ds(start, 8, stride=stride)


def snake_in(table, unit, c, values):
    return snake(values, rates(table, unit, IN, lane(c)))


def weave(main, others=(), own=(), lead=0):
    pace = 1 if len(main) == KERNEL else 2
    whole = sum(cost for cost, _ in others)
    spent, at = 0, 0
    for i, (_, step) in enumerate(main):
        step()
        if i // pace + 1 < len(own):
            late = own[i // pace + 1]
            run(late[i % pace :: pace])
        share = max(0, i + 1 - lead) / (len(main) - lead)
        while at < len(others) and (i + 1 == len(main) or spent < whole * share):
            spent += others[at][0]
            others[at][1]()
            at += 1


def run(steps):
    for _, step in steps:
        step()


def halves(channels):
    return slice(0, channels // 2), slice(channels // 2, channels)


def parts(frames):
    inner = (
        Part(0, [(8, frames // SEGMENTS - 5)]),
        Part(1, [(20, frames // SEGMENTS - 7)]),
        Part(2, [(48, frames // SEGMENTS - 11)]),
    )
    outer = (
        Part(0, [(-36, 3), (frames - 72, 7)]),
        Part(1, [(-28, 3), (frames - 100, 8)], plain=True),
        Part(2, [(0, 3), (frames - 128, 8)], plain=True),
    )
    return inner, outer


def place():
    return lax.axis_index("tm")


def edges_kernel(up_hbm, to_far, to_near, held, sems):
    frames = up_hbm.shape[1]
    copies = []
    for part in range(2):
        for end, row in enumerate((0, frames - SENT)):
            copies.append(
                pltpu.make_async_copy(
                    up_hbm.at[part, pl.ds(row, SENT)], held.at[part, end], sems.at[part, end]
                )
            )
    for copy in copies:
        copy.start()
    for copy in copies:
        copy.wait()
    odd = place() % 2 == 1
    for c in range(up_hbm.shape[2] // LANES):
        own_low, own_high = (held[0, end, :, lane(c)].astype(jnp.float32) for end in range(2))
        low, high = (held[1, end, :, lane(c)].astype(jnp.float32) for end in range(2))
        none = jnp.zeros((STRIDE, LANES), jnp.float32)
        to_next = jnp.concatenate([own_high[STRIDE:], none], axis=0) + high
        to_last = own_low + jnp.concatenate([none, low[:HALO]], axis=0)
        to_far[:, lane(c)] = jnp.where(odd, to_next, to_last).astype(jnp.bfloat16)
        to_near[:, lane(c)] = jnp.where(odd, to_last, to_next).astype(jnp.bfloat16)


def first_kernel(
    up, wide, point, alpha_in, beta_in, alpha_mid, beta_mid, x_rows, s_rows, tiles, table
):
    frames = up.shape[1]
    rows = []
    for alpha, beta in ((alpha_in, beta_in), (alpha_mid, beta_mid)):
        root = jnp.sqrt(1 / beta[...])
        rows += [alpha[...] / math.pi] + [root * coefficient for coefficient in SINE]
    for which, value in enumerate(rows + [wide[...], point[...]]):
        for unit in range(UNITS):
            row = unit * TABLE + which
            table[row : row + 1, :] = value[unit : unit + 1, :]
    for c in range(x_rows.shape[0]):
        later = up[1, :, lane(c)].astype(jnp.float32)
        none = jnp.zeros((STRIDE, LANES), jnp.float32)
        own = up[0, :, lane(c)].astype(jnp.float32)
        current = rounded(own + jnp.concatenate([none, later[: frames - STRIDE]], axis=0))
        table[UNITS * TABLE :, lane(c)] = later[frames - STRIDE :]
        x_rows[c, LEFT : LEFT + frames, :] = current
        early = frames - LATE
        s_rows[c, LEFT : LEFT + early, :] = snake_in(table, 0, c, current[:early])
    run(sum(parts(frames)[0][0].gather(s_rows, tiles), []))


def inner_kernel(frames, x_first, tiles, table, taps, middle, gated, s_late):
    part = parts(frames)[0][0]
    first, _ = halves(middle.shape[1])
    steps = part.conv(tiles, taps, middle)

    def late(c, row):
        start = LEFT + frames - LATE + row
        values = x_first[c, start : start + SEGMENTS, :]
        s_late[c, row : row + SEGMENTS, :] = snake_in(table, 0, c, values)

    late_steps = [
        (1, functools.partial(late, c, row))
        for c in range(x_first.shape[0])
        for row in range(0, LATE, SEGMENTS)
    ]
    weave(steps[:KERNEL], late_steps)
    weave(steps[KERNEL:], part.gate(middle, gated, table, first))


def outer_kernel(
    tracks,
    x_first, s_first, s_late, first_middle, first_gated, from_chip, from_far, table, taps, point,
    out,
    x_0, x_1, x_2, s_0, s_1, s_2, inner_tiles, outer_tiles, gated, gated_2, held, sems,
):
    inner, outer = parts(out.shape[0])

    def sums(*of):
        one = [pltpu.ACC(unit)((SEGMENTS, WIDTH), jnp.float32) for unit in range(2)]
        return [one] * (max(part.rows for part in of) // SEGMENTS)

    def scoped(inner_sums, outer_sums, last_sums, update_sums):
        outer_body(
            tracks,
            x_first, s_first, s_late, first_middle, first_gated, from_chip, from_far, table, taps,
            point, out,
            x_0, x_1, x_2, s_0, s_1, s_2, inner_tiles, outer_tiles, gated, gated_2, held, sems,
            inner_sums, outer_sums, last_sums, update_sums,
        )

    pl.run_scoped(
        scoped, sums(*inner[1:]), sums(*outer), sums(outer[2]), sums(*inner, *outer)
    )


def outer_body(
    tracks,
    x_first, s_first, s_late, first_middle, first_gated, from_chip, from_far, table, taps, point,
    out,
    x_0, x_1, x_2, s_0, s_1, s_2, inner_tiles, outer_tiles, gated, gated_2, held, sems,
    inner_sums, outer_sums, last_sums, update_sums,
):
    frames, channels = out.shape
    groups = x_0.shape[0]
    end_row = LEFT + frames
    odd = place() % 2 == 1
    is_first = place() == 0
    is_last = place() == tracks - 1
    inner, outer = parts(frames)
    both = halves(channels)

    def clear_outside(s_rows):
        def step(c):
            s_rows[c, 0:LEFT, :] = jnp.where(is_first, 0.0, s_rows[c, 0:LEFT, :])
            s_rows[c, end_row:, :] = jnp.where(is_last, 0.0, s_rows[c, end_row:, :])

        return [(10, functools.partial(step, c)) for c in range(groups)]

    copies = []

    def send(begin, end):
        def step():
            rows = pl.ds(begin, end - begin)
            copy = pltpu.make_async_copy(held.at[rows], out.at[rows], sems.at[len(copies)])
            copies.append(copy)
            copy.start()

        return step

    def store(begin, end):
        def step(c, row):
            rows = slice(LEFT + row, LEFT + row + SEGMENTS)
            held[row : row + SEGMENTS, lane(c)] = x_0[c, rows, :].astype(jnp.bfloat16)

        return [
            (2, functools.partial(step, c, row))
            for row in range(begin, end, SEGMENTS)
            for c in range(groups)
        ]

    matrix = Matrix()

    def after(part, sums, x_rows, x_next, s_next):
        return (
            part.gate_sums(sums, gated, table)
            + part.project(matrix, [(gated, columns) for columns in both], point, update_sums)
            + part.finish(update_sums, table, x_rows, x_next, s_next)
        )

    first_point = inner[0].project(
        matrix, [(first_gated, both[0]), (gated, both[1])], point, update_sums
    )
    run(first_point[:1])
    matrix.flush()

    low_end = LEFT + 2 * STRIDE
    kept = LEFT + outer[0].pieces[1][0] - 8
    for c in range(groups):
        chip = from_chip[:, lane(c)].astype(jnp.float32)
        far = from_far[:, lane(c)].astype(jnp.float32)
        before = jnp.where(odd, chip, far)
        behind = jnp.where(odd, far, chip)
        carried = jnp.where(is_first, 0.0, before[HALO:SENT])
        own_low = x_first[c, LEFT:low_end, :]
        low = jnp.concatenate(
            [before[:HALO], rounded(own_low[:STRIDE] + carried), own_low[STRIDE:]], axis=0
        )
        joint = rounded(behind[:STRIDE] + table[UNITS * TABLE :, lane(c)])
        high = jnp.concatenate([joint, behind[STRIDE:HALO]], axis=0)
        x_0[c, LEFT - HALO : low_end, :] = low
        s_0[c, LEFT - HALO : low_end, :] = snake_in(table, 0, c, low)
        x_0[c, kept:end_row, :] = x_first[c, kept:end_row, :]
        s_0[c, kept : end_row - LATE, :] = s_first[c, kept : end_row - LATE, :]
        s_0[c, end_row - LATE : end_row, :] = s_late[c]
        x_0[c, end_row : end_row + HALO, :] = high
        s_0[c, end_row : end_row + HALO, :] = snake_in(table, 0, c, high)
    run(clear_outside(s_0))
    lead = 1
    own = outer[0].gather(s_0, outer_tiles)
    run(own[0])
    coming = inner[1].gather(s_1, inner_tiles)
    weave(
        outer[0].conv_sums(matrix, outer_tiles, taps, outer_sums),
        inner[0].gate(first_middle, gated, table, both[1])
        + first_point[1:]
        + inner[0].finish(update_sums, table, x_first, x_1, s_1)
        + coming[0],
        own,
    )
    own, coming = coming, outer[1].gather(s_1, outer_tiles)
    weave(
        inner[1].conv_sums(matrix, inner_tiles, taps, inner_sums),
        after(outer[0], outer_sums, x_0, x_1, s_1) + clear_outside(s_1) + coming[0],
        own,
        lead,
    )
    own, coming = coming, inner[2].gather(s_2, inner_tiles)
    weave(
        outer[1].conv_sums(matrix, outer_tiles, taps, outer_sums),
        after(inner[1], inner_sums, x_1, x_2, s_2) + coming[0],
        own,
        lead,
    )
    own, coming = coming, outer[2].gather(s_2, outer_tiles)
    weave(
        inner[2].conv_sums(matrix, inner_tiles, taps, inner_sums),
        after(outer[1], outer_sums, x_1, x_2, s_2) + clear_outside(s_2) + coming[0],
        own,
        lead,
    )
    begin = inner[2].pieces[0][0]
    end = begin + inner[2].rows
    last = outer[2]
    finish = after(inner[2], inner_sums, x_2, x_0, None) + store(begin, end)
    finish.append((2, send(begin, end)))
    cut = len(finish) // 2
    sums = outer_sums, last_sums
    conv = [
        last.conv_sums(matrix, outer_tiles, taps, sums[n], columns)
        for n, columns in enumerate(both)
    ]
    point_steps = last.project(matrix, [(gated_2, columns) for columns in both], point, update_sums)
    weave(conv[0], finish[:cut], coming, lead)
    weave(conv[1], finish[cut:] + last.gate_columns(sums[0], gated_2, table, both[0]))
    run(point_steps[:1])
    run(last.gate_columns(sums[1], gated_2, table, both[1]))
    run(point_steps[1:])
    finish = last.finish_plain(update_sums, table, x_2, held)
    low_tiles = last.pieces[0][1]
    run(finish[:low_tiles] + [(2, send(0, begin))])
    run(finish[low_tiles:] + [(2, send(end, frames))])
    for copy in copies:
        copy.wait()


def swaps(groups, count):
    near, far = [], []
    for group in range(groups):
        for index in range(count):
            me = group * count + index
            near.append((me, group * count + (index ^ 1)))
            if index == 0 or index == count - 1:
                far.append((me, (group ^ 1) * count + index))
            else:
                far.append((me, me + 1 if index % 2 else me - 1))
    return near, far


VMEM = pl.BlockSpec(memory_space=pltpu.VMEM)
HBM = pl.BlockSpec(memory_space=pltpu.HBM)


def in_hbm(value):
    return pltpu.with_memory_space_constraint(value, pltpu.HBM)


VMEM = pl.BlockSpec(memory_space=pltpu.VMEM)
HBM = pl.BlockSpec(memory_space=pltpu.HBM)


def in_hbm(value):
    return pltpu.with_memory_space_constraint(value, pltpu.HBM)


def per_device(
    upsampled, taps, bias_wide, pointwise, bias_point, alpha_in, beta_in, alpha_mid, beta_mid
):
    frames, channels = upsampled.shape[1:]
    count = lax.axis_size("tm")
    near, far = swaps(lax.axis_size("grp"), count)
    groups = channels // LANES
    rows = frames + 2 * LEFT
    half = jnp.bfloat16
    params = (bias_wide, bias_point, alpha_in, beta_in, alpha_mid, beta_mid)
    limit = pltpu.CompilerParams(vmem_limit_bytes=16 * 2**20)

    sent = jax.ShapeDtypeStruct((SENT, channels), half)
    to_far, to_near = pl.pallas_call(
        edges_kernel,
        out_shape=(sent, sent),
        in_specs=[HBM],
        out_specs=(VMEM,) * 2,
        scratch_shapes=[
            pltpu.VMEM((2, 2, SENT, channels), half),
            pltpu.SemaphoreType.DMA((2, 2)),
        ],
        compiler_params=limit,
        cost_estimate=pl.CostEstimate(
            flops=6 * 10**9, bytes_accessed=upsampled.size * 2, transcendentals=0
        ),
        name="edges",
    )(in_hbm(upsampled))

    from_far = lax.ppermute(to_far, ("grp", "tm"), far)
    from_chip = lax.ppermute(to_near, ("grp", "tm"), near)

    inner, outer = parts(frames)
    natural = (groups, rows, LANES)
    single = jnp.float32

    def tiles(*of):
        return max(part.tiles for part in of) * SEGMENTS, channels

    def most(*of):
        return max(part.rows for part in of), channels

    x_first, s_first, first_tiles, table = pl.pallas_call(
        first_kernel,
        out_shape=(
            jax.ShapeDtypeStruct(natural, single),
            jax.ShapeDtypeStruct(natural, single),
            jax.ShapeDtypeStruct(tiles(inner[0]), half),
            jax.ShapeDtypeStruct((UNITS * TABLE + STRIDE, channels), single),
        ),
        in_specs=[VMEM] * 7,
        out_specs=(VMEM,) * 4,
        compiler_params=limit,
        name="first",
    )(upsampled, *params)

    first_middle, first_gated, s_late = pl.pallas_call(
        functools.partial(inner_kernel, frames),
        out_shape=(
            jax.ShapeDtypeStruct(most(inner[0]), single),
            jax.ShapeDtypeStruct(most(inner[0]), half),
            jax.ShapeDtypeStruct((groups, LATE, LANES), single),
        ),
        in_specs=[VMEM] * 4,
        out_specs=(VMEM,) * 3,
        compiler_params=limit,
        cost_estimate=pl.CostEstimate(
            flops=2 * KERNEL * inner[0].rows * channels**2,
            bytes_accessed=taps.size * 2,
            transcendentals=0,
        ),
        name="inner",
    )(x_first, first_tiles, table, taps)

    return pl.pallas_call(
        functools.partial(outer_kernel, count),
        out_shape=jax.ShapeDtypeStruct((frames, channels), half),
        in_specs=[VMEM] * 10,
        out_specs=HBM,
        scratch_shapes=[pltpu.VMEM(natural, single)] * 6
        + [
            pltpu.VMEM(tiles(*inner[1:]), half),
            pltpu.VMEM(tiles(*outer), half),
            pltpu.VMEM(most(*inner, *outer), half),
            pltpu.VMEM(most(outer[2]), half),
            pltpu.VMEM((frames, channels), half),
            pltpu.SemaphoreType.DMA((3,)),
        ],
        compiler_params=pltpu.CompilerParams(vmem_limit_bytes=24 * 2**20),
        name="outer",
    )(
        x_first, s_first, s_late, first_middle, first_gated, from_chip, from_far,
        table, taps, pointwise,
    )


def solution(mesh):
    placed = (P(None, ("grp", "tm"), None), P(), P(), P(), P(), P(), P(), P(), P())
    return jax.shard_map(
        per_device, mesh=mesh, in_specs=placed, out_specs=P(("grp", "tm"), None), check_vma=False
    )
```

```python
import functools
import math

import jax
import jax.numpy as jnp
from jax import lax
from jax.experimental import pallas as pl
from jax.experimental.pallas import tpu as pltpu
from jax.sharding import PartitionSpec as P

KERNEL = 7
STRIDE = 8
UNITS = 3
DILATIONS = (1, 3, 9)
LANES = 128
LEFT = 48
SENT = 48
HALO = 40
LATE = 64
SEGMENTS = 16
TABLE = 16
IN, MID, WIDE, POINT = 0, 5, 10, 11

SINE = (3.141582022, -5.167142795, 2.541899018, -0.5546361724)


def snake(values, rates):
    turns = values * rates[0]
    rest = turns - jnp.round(turns)
    square = rest * rest
    sine = rates[-1]
    for coefficient in rates[-2:0:-1]:
        sine = sine * square + coefficient
    sine = sine * rest
    return values + sine * sine


def rounded(values):
    return values.astype(jnp.bfloat16).astype(jnp.float32)


def lane(c):
    return slice(c * LANES, (c + 1) * LANES)


def entry(table, unit, which, lanes=slice(None)):
    row = unit * TABLE + which
    return table[row : row + 1, lanes]


WIDTH = 256


def rates(table, unit, which, lanes):
    return [entry(table, unit, which + i, lanes) for i in range(5)]


class Matrix:
    def __init__(self):
        self.count = 0
        self.staged = None

    def tile(self, weights, rows, sums):
        register = self.count % 2
        self.count += 1
        for unit in range(2):
            pltpu.matmul_push_rhs(weights(unit), register, unit)
        self.flush()
        self.staged = register, rows, sums

    def flush(self):
        if self.staged is None:
            return
        register, rows, sums = self.staged
        self.staged = None
        for i, pair in enumerate(sums):
            for unit in range(2):
                load = register if i == 0 else None
                pltpu.matmul_acc_lhs(pair[unit], rows(unit, i), load_staged_rhs=load)


class Part:
    def __init__(self, unit, pieces, plain=False):
        self.unit = unit
        self.plain = plain
        self.dilation = DILATIONS[unit]
        self.pieces = pieces
        self.rows = SEGMENTS * sum(length for _, length in pieces)
        if plain:
            self.tiles = KERNEL * self.rows // SEGMENTS
        else:
            self.tiles = sum(length + 6 * self.dilation for _, length in pieces)

    def starts(self, first, j, length):
        if self.plain:
            start = LEFT + first + SEGMENTS * j
            return (start, start + 8), 1
        start = LEFT + first + j
        return (start, start + 8 * length), length

    def gather(self, s_rows, tiles):
        steps = [[] for _ in range(KERNEL)]

        def step(at, first, j, length):
            rows = slice(at * SEGMENTS, (at + 1) * SEGMENTS)
            starts, stride = self.starts(first, j, length)
            for c in range(s_rows.shape[0]):
                both = [s_rows[c, run_of(start, stride), :] for start in starts]
                tiles[rows, lane(c)] = jnp.concatenate(both, axis=0).astype(jnp.bfloat16)

        reach = 3 * self.dilation
        for k in range(KERNEL):
            at = 0
            for first, length in self.pieces:
                if self.plain:
                    away = first + (k - 3) * self.dilation
                    new = [(k * self.rows // SEGMENTS + at + j, away, j) for j in range(length)]
                    at += length
                else:
                    begin = length + (k - 1) * self.dilation if k else 0
                    end = length + k * self.dilation
                    new = [(at + j, first - reach, j) for j in range(begin, end)]
                    at += length + 2 * reach
                for tile, start, j in new:
                    steps[k].append((10, functools.partial(step, tile, start, j, length)))
        return steps

    def window(self, tiles, k):
        at, found = 0, []
        for _, length in self.pieces:
            row = (at + k * self.dilation) * SEGMENTS
            found.append(tiles[row : row + length * SEGMENTS, :])
            at += length + 6 * self.dilation
        return found[0] if len(found) == 1 else jnp.concatenate(found, axis=0)

    def conv(self, tiles, taps, middle):
        channels = middle.shape[1]
        total = [None]

        def step(columns, k):
            product = jnp.dot(
                self.window(tiles, k),
                taps[self.unit, k, :, columns],
                preferred_element_type=jnp.float32,
            )
            total[0] = product if k == 0 else total[0] + product
            if k == KERNEL - 1:
                middle[: self.rows, columns] = total[0]

        return [
            (1, functools.partial(step, columns, k))
            for columns in halves(channels)
            for k in range(KERNEL)
        ]

    def conv_sums(self, matrix, tiles, taps, sums, columns=None):
        places, at = [], 0
        for _, length in self.pieces:
            places += range(at, at + length)
            at += length + (0 if self.plain else 6 * self.dilation)
        away = len(places) if self.plain else self.dilation

        both = halves(taps.shape[2])

        def rows(k, inputs, i):
            row = (places[i] + k * away) * SEGMENTS
            return tiles[row : row + SEGMENTS, inputs]

        def step(k, inputs):
            matrix.tile(
                lambda unit: taps[self.unit, k, inputs, both[unit]],
                lambda unit, i: rows(k, inputs, i),
                sums[: len(places)],
            )

        def column_step(k):
            matrix.tile(
                lambda unit: taps[self.unit, k, both[unit], columns],
                lambda unit, i: rows(k, both[unit], i),
                sums[: len(places)],
            )

        if columns is not None:
            return [(1, functools.partial(column_step, k)) for k in range(KERNEL)]
        steps = [
            (1, functools.partial(step, k, inputs)) for k in range(KERNEL) for inputs in both
        ]
        return steps + [(1, matrix.flush)]

    def gate_values(self, values, gated, table, columns):
        gated_values = snake(
            values + entry(table, self.unit, WIDE, columns),
            rates(table, self.unit, MID, columns),
        )
        return gated_values.astype(jnp.bfloat16)

    def gate(self, middle, gated, table, columns):
        def step(rows):
            gated[rows, columns] = self.gate_values(middle[rows, columns], gated, table, columns)

        return [
            (20, functools.partial(step, slice(row, row + SEGMENTS)))
            for row in range(0, self.rows, SEGMENTS)
        ]

    def gate_sums(self, sums, gated, table):
        def step(i):
            rows = slice(i * SEGMENTS, (i + 1) * SEGMENTS)
            for unit, columns in enumerate(halves(gated.shape[1])):
                values = pltpu.matmul_pop(sums[i][unit])
                gated[rows, columns] = self.gate_values(values, gated, table, columns)

        return [(20, functools.partial(step, i)) for i in range(self.rows // SEGMENTS)]

    def finish_plain(self, sums, table, x_rows, out):
        steps = []

        def step(i, first, j):
            row = first + SEGMENTS * j
            for c in range(x_rows.shape[0]):
                unit, group = divmod(c, WIDTH // LANES)
                if group == 0:
                    update = pltpu.matmul_pop(sums[i][unit])
                change = update[:, lane(group)] + entry(table, self.unit, POINT, lane(c))
                current = x_rows[c, LEFT + row : LEFT + row + SEGMENTS, :] + change
                out[row : row + SEGMENTS, lane(c)] = current.astype(jnp.bfloat16)

        for first, length in self.pieces:
            for j in range(length):
                steps.append((20, functools.partial(step, len(steps), first, j)))
        return steps

    def gate_columns(self, sums, gated, table, columns):
        def step(i):
            rows = slice(i * SEGMENTS, (i + 1) * SEGMENTS)
            values = pltpu.matmul_pop(sums[i][0]) + pltpu.matmul_pop(sums[i][1])
            gated[rows, columns] = self.gate_values(values, gated, table, columns)

        return [(20, functools.partial(step, i)) for i in range(self.rows // SEGMENTS)]

    def project(self, matrix, sources, point, sums):
        def rows(gated, columns, i):
            return gated[i * SEGMENTS : (i + 1) * SEGMENTS, columns]

        both = halves(point.shape[2])

        def step(gated, inputs):
            matrix.tile(
                lambda unit: point[self.unit, inputs, both[unit]],
                lambda unit, i: rows(gated, inputs, i),
                sums[: self.rows // SEGMENTS],
            )

        steps = [(5, functools.partial(step, gated, columns)) for gated, columns in sources]
        return steps + [(5, matrix.flush)]

    def finish(self, sums, table, x_rows, x_next, s_next=None):
        steps = []

        def step(i, first, j, length):
            starts, stride = self.starts(first, j, length)
            update = [pltpu.matmul_pop(sums[i][unit]) for unit in range(2)]
            for half in range(2):
                where = run_of(starts[half], stride)
                rows = slice(half * 8, half * 8 + 8)
                for c in range(x_rows.shape[0]):
                    unit, group = divmod(c, WIDTH // LANES)
                    change = update[unit][rows, lane(group)] + entry(
                        table, self.unit, POINT, lane(c)
                    )
                    current = rounded(x_rows[c, where, :] + change)
                    x_next[c, where, :] = current
                    if s_next is not None:
                        s_next[c, where, :] = snake_in(table, self.unit + 1, c, current)

        for first, length in self.pieces:
            for j in range(length):
                cost = 25 if s_next is None else 35
                steps.append(
                    (cost, functools.partial(step, len(steps), first, j, length))
                )
        return steps


def run_of(start, stride):
    return pl.ds(start, 8) if stride == 1 else pl.ds(start, 8, stride=stride)


def snake_in(table, unit, c, values):
    return snake(values, rates(table, unit, IN, lane(c)))


def weave(main, others=(), own=(), lead=0):
    pace = 1 if len(main) == KERNEL else 2
    whole = sum(cost for cost, _ in others)
    spent, at = 0, 0
    for i, (_, step) in enumerate(main):
        step()
        if i // pace + 1 < len(own):
            late = own[i // pace + 1]
            run(late[i % pace :: pace])
        share = max(0, i + 1 - lead) / (len(main) - lead)
        while at < len(others) and (i + 1 == len(main) or spent < whole * share):
            spent += others[at][0]
            others[at][1]()
            at += 1


def run(steps):
    for _, step in steps:
        step()


def halves(channels):
    return slice(0, channels // 2), slice(channels // 2, channels)


def parts(frames):
    inner = (
        Part(0, [(8, frames // SEGMENTS - 5)]),
        Part(1, [(20, frames // SEGMENTS - 7)]),
        Part(2, [(48, frames // SEGMENTS - 11)]),
    )
    outer = (
        Part(0, [(-36, 3), (frames - 72, 7)]),
        Part(1, [(-28, 3), (frames - 100, 8)], plain=True),
        Part(2, [(0, 3), (frames - 128, 8)], plain=True),
    )
    return inner, outer


def place():
    return lax.axis_index("tm")


def edges_kernel(up_hbm, to_far, to_near, held, sems):
    frames = up_hbm.shape[1]
    copies = []
    for part in range(2):
        for end, row in enumerate((0, frames - SENT)):
            copies.append(
                pltpu.make_async_copy(
                    up_hbm.at[part, pl.ds(row, SENT)], held.at[part, end], sems.at[part, end]
                )
            )
    for copy in copies:
        copy.start()
    for copy in copies:
        copy.wait()
    odd = place() % 2 == 1
    for c in range(up_hbm.shape[2] // LANES):
        own_low, own_high = (held[0, end, :, lane(c)].astype(jnp.float32) for end in range(2))
        low, high = (held[1, end, :, lane(c)].astype(jnp.float32) for end in range(2))
        none = jnp.zeros((STRIDE, LANES), jnp.float32)
        to_next = jnp.concatenate([own_high[STRIDE:], none], axis=0) + high
        to_last = own_low + jnp.concatenate([none, low[:HALO]], axis=0)
        to_far[:, lane(c)] = jnp.where(odd, to_next, to_last).astype(jnp.bfloat16)
        to_near[:, lane(c)] = jnp.where(odd, to_last, to_next).astype(jnp.bfloat16)


def first_kernel(
    up, wide, point, alpha_in, beta_in, alpha_mid, beta_mid, x_rows, s_rows, tiles, table
):
    frames = up.shape[1]
    rows = []
    for alpha, beta in ((alpha_in, beta_in), (alpha_mid, beta_mid)):
        root = jnp.sqrt(1 / beta[...])
        rows += [alpha[...] / math.pi] + [root * coefficient for coefficient in SINE]
    for which, value in enumerate(rows + [wide[...], point[...]]):
        for unit in range(UNITS):
            row = unit * TABLE + which
            table[row : row + 1, :] = value[unit : unit + 1, :]
    for c in range(x_rows.shape[0]):
        later = up[1, :, lane(c)].astype(jnp.float32)
        none = jnp.zeros((STRIDE, LANES), jnp.float32)
        own = up[0, :, lane(c)].astype(jnp.float32)
        current = rounded(own + jnp.concatenate([none, later[: frames - STRIDE]], axis=0))
        table[UNITS * TABLE :, lane(c)] = later[frames - STRIDE :]
        x_rows[c, LEFT : LEFT + frames, :] = current
        early = frames - LATE
        s_rows[c, LEFT : LEFT + early, :] = snake_in(table, 0, c, current[:early])
    run(sum(parts(frames)[0][0].gather(s_rows, tiles), []))


def inner_kernel(frames, x_first, tiles, table, taps, middle, gated, s_late):
    part = parts(frames)[0][0]
    first, _ = halves(middle.shape[1])
    steps = part.conv(tiles, taps, middle)

    def late(c, row):
        start = LEFT + frames - LATE + row
        values = x_first[c, start : start + SEGMENTS, :]
        s_late[c, row : row + SEGMENTS, :] = snake_in(table, 0, c, values)

    late_steps = [
        (1, functools.partial(late, c, row))
        for c in range(x_first.shape[0])
        for row in range(0, LATE, SEGMENTS)
    ]
    weave(steps[:KERNEL], late_steps)
    weave(steps[KERNEL:], part.gate(middle, gated, table, first))


def outer_kernel(
    tracks,
    x_first, s_first, s_late, first_middle, first_gated, from_chip, from_far, table, taps, point,
    out,
    x_0, x_1, x_2, s_0, s_1, s_2, inner_tiles, outer_tiles, gated, gated_2, held, sems,
):
    inner, outer = parts(out.shape[0])

    def sums(*of):
        one = [pltpu.ACC(unit)((SEGMENTS, WIDTH), jnp.float32) for unit in range(2)]
        return [one] * (max(part.rows for part in of) // SEGMENTS)

    def scoped(inner_sums, outer_sums, last_sums, update_sums):
        outer_body(
            tracks,
            x_first, s_first, s_late, first_middle, first_gated, from_chip, from_far, table, taps,
            point, out,
            x_0, x_1, x_2, s_0, s_1, s_2, inner_tiles, outer_tiles, gated, gated_2, held, sems,
            inner_sums, outer_sums, last_sums, update_sums,
        )

    pl.run_scoped(
        scoped, sums(*inner[1:]), sums(*outer), sums(outer[2]), sums(*inner, *outer)
    )


def outer_body(
    tracks,
    x_first, s_first, s_late, first_middle, first_gated, from_chip, from_far, table, taps, point,
    out,
    x_0, x_1, x_2, s_0, s_1, s_2, inner_tiles, outer_tiles, gated, gated_2, held, sems,
    inner_sums, outer_sums, last_sums, update_sums,
):
    frames, channels = out.shape
    groups = x_0.shape[0]
    end_row = LEFT + frames
    odd = place() % 2 == 1
    is_first = place() == 0
    is_last = place() == tracks - 1
    inner, outer = parts(frames)
    both = halves(channels)

    def clear_outside(s_rows):
        def step(c):
            s_rows[c, 0:LEFT, :] = jnp.where(is_first, 0.0, s_rows[c, 0:LEFT, :])
            s_rows[c, end_row:, :] = jnp.where(is_last, 0.0, s_rows[c, end_row:, :])

        return [(10, functools.partial(step, c)) for c in range(groups)]

    copies = []

    def send(begin, end):
        def step():
            rows = pl.ds(begin, end - begin)
            copy = pltpu.make_async_copy(held.at[rows], out.at[rows], sems.at[len(copies)])
            copies.append(copy)
            copy.start()

        return step

    def store(begin, end):
        def step(c, row):
            rows = slice(LEFT + row, LEFT + row + SEGMENTS)
            held[row : row + SEGMENTS, lane(c)] = x_0[c, rows, :].astype(jnp.bfloat16)

        return [
            (2, functools.partial(step, c, row))
            for row in range(begin, end, SEGMENTS)
            for c in range(groups)
        ]

    matrix = Matrix()

    def after(part, sums, x_rows, x_next, s_next):
        return (
            part.gate_sums(sums, gated, table)
            + part.project(matrix, [(gated, columns) for columns in both], point, update_sums)
            + part.finish(update_sums, table, x_rows, x_next, s_next)
        )

    first_point = inner[0].project(
        matrix, [(first_gated, both[0]), (gated, both[1])], point, update_sums
    )
    run(first_point[:1])
    matrix.flush()

    low_end = LEFT + 2 * STRIDE
    kept = LEFT + outer[0].pieces[1][0] - 8
    for c in range(groups):
        chip = from_chip[:, lane(c)].astype(jnp.float32)
        far = from_far[:, lane(c)].astype(jnp.float32)
        before = jnp.where(odd, chip, far)
        behind = jnp.where(odd, far, chip)
        carried = jnp.where(is_first, 0.0, before[HALO:SENT])
        own_low = x_first[c, LEFT:low_end, :]
        low = jnp.concatenate(
            [before[:HALO], rounded(own_low[:STRIDE] + carried), own_low[STRIDE:]], axis=0
        )
        joint = rounded(behind[:STRIDE] + table[UNITS * TABLE :, lane(c)])
        high = jnp.concatenate([joint, behind[STRIDE:HALO]], axis=0)
        x_0[c, LEFT - HALO : low_end, :] = low
        s_0[c, LEFT - HALO : low_end, :] = snake_in(table, 0, c, low)
        x_0[c, kept:end_row, :] = x_first[c, kept:end_row, :]
        s_0[c, kept : end_row - LATE, :] = s_first[c, kept : end_row - LATE, :]
        s_0[c, end_row - LATE : end_row, :] = s_late[c]
        x_0[c, end_row : end_row + HALO, :] = high
        s_0[c, end_row : end_row + HALO, :] = snake_in(table, 0, c, high)
    run(clear_outside(s_0))
    lead = 1
    own = outer[0].gather(s_0, outer_tiles)
    run(own[0])
    coming = inner[1].gather(s_1, inner_tiles)
    weave(
        outer[0].conv_sums(matrix, outer_tiles, taps, outer_sums),
        inner[0].gate(first_middle, gated, table, both[1])
        + first_point[1:]
        + inner[0].finish(update_sums, table, x_first, x_1, s_1)
        + coming[0],
        own,
    )
    own, coming = coming, outer[1].gather(s_1, outer_tiles)
    weave(
        inner[1].conv_sums(matrix, inner_tiles, taps, inner_sums),
        after(outer[0], outer_sums, x_0, x_1, s_1) + clear_outside(s_1) + coming[0],
        own,
        lead,
    )
    own, coming = coming, inner[2].gather(s_2, inner_tiles)
    weave(
        outer[1].conv_sums(matrix, outer_tiles, taps, outer_sums),
        after(inner[1], inner_sums, x_1, x_2, s_2) + coming[0],
        own,
        lead,
    )
    own, coming = coming, outer[2].gather(s_2, outer_tiles)
    weave(
        inner[2].conv_sums(matrix, inner_tiles, taps, inner_sums),
        after(outer[1], outer_sums, x_1, x_2, s_2) + clear_outside(s_2) + coming[0],
        own,
        lead,
    )
    begin = inner[2].pieces[0][0]
    end = begin + inner[2].rows
    last = outer[2]
    finish = after(inner[2], inner_sums, x_2, x_0, None) + store(begin, end)
    finish.append((2, send(begin, end)))
    cut = len(finish) // 2
    sums = outer_sums, last_sums
    conv = [
        last.conv_sums(matrix, outer_tiles, taps, sums[n], columns)
        for n, columns in enumerate(both)
    ]
    point_steps = last.project(matrix, [(gated_2, columns) for columns in both], point, update_sums)
    weave(conv[0], finish[:cut], coming, lead)
    weave(conv[1], finish[cut:] + last.gate_columns(sums[0], gated_2, table, both[0]))
    run(point_steps[:1])
    run(last.gate_columns(sums[1], gated_2, table, both[1]))
    run(point_steps[1:])
    finish = last.finish_plain(update_sums, table, x_2, held)
    low_tiles = last.pieces[0][1]
    run(finish[:low_tiles] + [(2, send(0, begin))])
    middle_tiles = low_tiles + last.pieces[1][1] // 2
    middle_row = end + last.pieces[1][1] // 2 * SEGMENTS
    run(finish[low_tiles:middle_tiles] + [(2, send(end, middle_row))])
    run(finish[middle_tiles:] + [(2, send(middle_row, frames))])
    for copy in copies:
        copy.wait()


def swaps(groups, count):
    near, far = [], []
    for group in range(groups):
        for index in range(count):
            me = group * count + index
            near.append((me, group * count + (index ^ 1)))
            if index == 0 or index == count - 1:
                far.append((me, (group ^ 1) * count + index))
            else:
                far.append((me, me + 1 if index % 2 else me - 1))
    return near, far


VMEM = pl.BlockSpec(memory_space=pltpu.VMEM)
HBM = pl.BlockSpec(memory_space=pltpu.HBM)


def in_hbm(value):
    return pltpu.with_memory_space_constraint(value, pltpu.HBM)


VMEM = pl.BlockSpec(memory_space=pltpu.VMEM)
HBM = pl.BlockSpec(memory_space=pltpu.HBM)


def in_hbm(value):
    return pltpu.with_memory_space_constraint(value, pltpu.HBM)


def per_device(
    upsampled, taps, bias_wide, pointwise, bias_point, alpha_in, beta_in, alpha_mid, beta_mid
):
    frames, channels = upsampled.shape[1:]
    count = lax.axis_size("tm")
    near, far = swaps(lax.axis_size("grp"), count)
    groups = channels // LANES
    rows = frames + 2 * LEFT
    half = jnp.bfloat16
    params = (bias_wide, bias_point, alpha_in, beta_in, alpha_mid, beta_mid)
    limit = pltpu.CompilerParams(vmem_limit_bytes=16 * 2**20)

    sent = jax.ShapeDtypeStruct((SENT, channels), half)
    to_far, to_near = pl.pallas_call(
        edges_kernel,
        out_shape=(sent, sent),
        in_specs=[HBM],
        out_specs=(VMEM,) * 2,
        scratch_shapes=[
            pltpu.VMEM((2, 2, SENT, channels), half),
            pltpu.SemaphoreType.DMA((2, 2)),
        ],
        compiler_params=limit,
        cost_estimate=pl.CostEstimate(
            flops=6 * 10**9, bytes_accessed=upsampled.size * 2, transcendentals=0
        ),
        name="edges",
    )(in_hbm(upsampled))

    from_far = lax.ppermute(to_far, ("grp", "tm"), far)
    from_chip = lax.ppermute(to_near, ("grp", "tm"), near)

    inner, outer = parts(frames)
    natural = (groups, rows, LANES)
    single = jnp.float32

    def tiles(*of):
        return max(part.tiles for part in of) * SEGMENTS, channels

    def most(*of):
        return max(part.rows for part in of), channels

    x_first, s_first, first_tiles, table = pl.pallas_call(
        first_kernel,
        out_shape=(
            jax.ShapeDtypeStruct(natural, single),
            jax.ShapeDtypeStruct(natural, single),
            jax.ShapeDtypeStruct(tiles(inner[0]), half),
            jax.ShapeDtypeStruct((UNITS * TABLE + STRIDE, channels), single),
        ),
        in_specs=[VMEM] * 7,
        out_specs=(VMEM,) * 4,
        compiler_params=limit,
        name="first",
    )(upsampled, *params)

    first_middle, first_gated, s_late = pl.pallas_call(
        functools.partial(inner_kernel, frames),
        out_shape=(
            jax.ShapeDtypeStruct(most(inner[0]), single),
            jax.ShapeDtypeStruct(most(inner[0]), half),
            jax.ShapeDtypeStruct((groups, LATE, LANES), single),
        ),
        in_specs=[VMEM] * 4,
        out_specs=(VMEM,) * 3,
        compiler_params=limit,
        cost_estimate=pl.CostEstimate(
            flops=2 * KERNEL * inner[0].rows * channels**2,
            bytes_accessed=taps.size * 2,
            transcendentals=0,
        ),
        name="inner",
    )(x_first, first_tiles, table, taps)

    return pl.pallas_call(
        functools.partial(outer_kernel, count),
        out_shape=jax.ShapeDtypeStruct((frames, channels), half),
        in_specs=[VMEM] * 10,
        out_specs=HBM,
        scratch_shapes=[pltpu.VMEM(natural, single)] * 6
        + [
            pltpu.VMEM(tiles(*inner[1:]), half),
            pltpu.VMEM(tiles(*outer), half),
            pltpu.VMEM(most(*inner, *outer), half),
            pltpu.VMEM(most(outer[2]), half),
            pltpu.VMEM((frames, channels), half),
            pltpu.SemaphoreType.DMA((4,)),
        ],
        compiler_params=pltpu.CompilerParams(vmem_limit_bytes=24 * 2**20),
        name="outer",
    )(
        x_first, s_first, s_late, first_middle, first_gated, from_chip, from_far,
        table, taps, pointwise,
    )


def solution(mesh):
    placed = (P(None, ("grp", "tm"), None), P(), P(), P(), P(), P(), P(), P(), P())
    return jax.shard_map(
        per_device, mesh=mesh, in_specs=placed, out_specs=P(("grp", "tm"), None), check_vma=False
    )
```
